512 devices in a mesh: ctx: 32 (over z, core), uly: 16 (over x, y).
Axes of the slice: x: 4, y: 4, z: 16, core: 2. Of those that a mesh axis runs over, the one named last changes fastest.
Arguments:
- queries: bfloat16 [32768, 12288], P(('ctx', 'uly')), may hold values from -8 to 8
- latent: bfloat16 [32768, 576], P(('ctx', 'uly')), may hold values from -8 to 8
- key_up: bfloat16 [512, 8192], P(None, 'uly'), may hold values from -0.25 to 0.25
- value_up: bfloat16 [512, 8192], P(None, 'uly'), may hold values from -0.25 to 0.25
- doc_lengths: int32 [128], replicated, may hold values from 1 to 1024, 32768 in all
Outputs:
- head_out: bfloat16 [32768, 8192], P(('ctx', 'uly'))
The draws below stay inside these ranges and needn't reach their ends.
Inputs may be any that keep to these rules, and one draw needn't show every extreme that they name: `doc_lengths`: the lengths sum to 32768; the longest document has exactly 1024 tokens.
All inputs are finite; a program needn't handle non-finite values.
Results may differ from the reference program's by a relative error of at most 0.0065.
Values may be sent and summed in bfloat16 or wider, within the bound.
No kernel may reach another device: no remote copies, remote signals or barrier semaphores. Data moves between devices by JAX's collectives and lax.ppermute only.
A program may use at most 64 MiB of HBM per device.

```python
import math
import jax
import jax.numpy as jnp
import numpy as np
from jax import lax

HEADS = 64
LATENT = 512
ROPE = 64
NOPE = 128
VDIM = 128
BLOCK = 1024
TOKENS = 32768
NDOCS = 128


def draw_latent(key, part):
    key = jax.random.fold_in(key, 3)
    values = jnp.clip(jax.random.normal(key, (TOKENS, LATENT + ROPE)), -6.0, 6.0)
    return values.astype(jnp.bfloat16)


def draw_queries(key, part):
    key = jax.random.fold_in(key, 5)
    values = jnp.clip(jax.random.normal(key, (TOKENS, HEADS, NOPE + ROPE)), -6.0, 6.0)
    return values.reshape(TOKENS, HEADS * (NOPE + ROPE)).astype(jnp.bfloat16)


def shard_levels(own_key, extent, split, low, largest):
    def one(axis_at, parts):
        draws = jax.random.uniform(jax.random.fold_in(jax.random.fold_in(own_key, 6), axis_at), (parts,), jnp.float32, low / len(split), largest / len(split))
        return jnp.repeat(jnp.exp(draws), extent[axis_at] // parts).reshape((-1,) + (1,) * (len(extent) - axis_at - 1))

    factor_of = one(*split[0])
    for cut in split[1:]:
        factor_of = factor_of * one(*cut)
    return factor_of


def split_up(number_of, total, most, lean):
    weights = [(1 << 20) // math.isqrt(rank ** lean) + 1 for rank in range(2, number_of + 1)]
    rest, holding = total - most - (number_of - 1), [1] * (number_of - 1)
    while rest > 0:
        movable = [i for i in range(number_of - 1) if holding[i] < most]
        whole, budget = sum([weights[i] for i in movable]), rest
        for i in movable:
            more = min(most - holding[i], max(1, budget * weights[i] // whole), rest)
            holding[i] = holding[i] + more
            rest = rest - more
    return np.array([most] + holding)


def ragged(rng, amount, total, bound, skew):
    if amount == 2:
        one = jax.random.randint(rng, (), max(1, total - bound), min(bound, total - 1) + 1)
        return jnp.stack([one, total - one])
    lengths = jnp.asarray(split_up(amount, total, bound, skew), jnp.int32)
    twos = (amount - 1) // 2
    donor, taker = lengths[1:1 + 2 * twos:2], lengths[2:2 + 2 * twos:2]
    room = jnp.minimum(donor - 1, bound - taker)
    passed = jax.random.randint(jax.random.fold_in(rng, 1), (twos,), 0, 1 << 20) % (room + 1)
    lengths = lengths.at[1:1 + 2 * twos:2].set(donor - passed).at[2:2 + 2 * twos:2].set(taker + passed)
    return lengths[jax.random.permutation(jax.random.fold_in(rng, 2), amount)]


def bell_draw(own_key, extent, width, reach, shards=(), kind=jnp.bfloat16):
    level = shard_levels(own_key, extent, shards, -0.22, 0.18) if shards else 1.0
    drawn = jax.random.normal(own_key, extent, jnp.float32) * width * level
    return jnp.minimum(jnp.maximum(drawn, -reach), reach).astype(kind)


def setup_inputs(seed: int = 0) -> dict:
    seeds = jax.random.split(jax.random.key(seed), 6)
    return {
        "queries": draw_queries(jax.random.fold_in(seeds[5], 71), 0),
        "latent": draw_latent(jax.random.fold_in(seeds[5], 71), 0),
        "key_up": bell_draw(seeds[2], (LATENT, HEADS * NOPE), LATENT ** -0.5, 0.25, ((1, 16),)),
        "value_up": bell_draw(seeds[3], (LATENT, HEADS * VDIM), LATENT ** -0.5, 0.25, ((1, 16),)),
        "doc_lengths": ragged(seeds[4], NDOCS, TOKENS, BLOCK, 2).astype(jnp.int32),
    }


def doc_first(doc_lengths, position):
    doc_ends = jnp.cumsum(doc_lengths).astype(jnp.int32)
    starts = (doc_ends - doc_lengths).astype(jnp.int32)
    before = starts[None, :] <= position[:, None]
    return lax.optimization_barrier(jnp.max(jnp.where(before, starts[None, :], 0), axis=1)).astype(jnp.int32)

def reference(queries, latent, key_up, value_up, doc_lengths):
    score_scale = 1.0 / math.sqrt(NOPE + ROPE)
    compact = latent[:, :LATENT]
    key_rows = jnp.dot(compact, key_up, preferred_element_type=jnp.float32).astype(jnp.bfloat16)
    value_rows = jnp.dot(compact, value_up, preferred_element_type=jnp.float32).astype(jnp.bfloat16)
    key_ext = jnp.concatenate([jnp.zeros((BLOCK, HEADS * NOPE), jnp.bfloat16), key_rows], axis=0)
    value_ext = jnp.concatenate([jnp.zeros((BLOCK, HEADS * VDIM), jnp.bfloat16), value_rows], axis=0)
    rope_ext = jnp.concatenate([jnp.zeros((BLOCK, ROPE), jnp.bfloat16), latent[:, LATENT:]], axis=0)
    position = jnp.arange(TOKENS, dtype=jnp.int32)
    first_key = doc_first(doc_lengths, position)

    def one_block(block_id):
        begin = (block_id * BLOCK).astype(jnp.int32)
        query_block = lax.dynamic_slice_in_dim(queries, begin, BLOCK, 0).astype(jnp.float32)
        query_block = query_block.reshape(BLOCK, HEADS, NOPE + ROPE)
        key_block = lax.dynamic_slice_in_dim(key_ext, begin, 2 * BLOCK, 0).astype(jnp.float32)
        key_block = key_block.reshape(2 * BLOCK, HEADS, NOPE)
        value_block = lax.dynamic_slice_in_dim(value_ext, begin, 2 * BLOCK, 0).astype(jnp.float32)
        value_block = value_block.reshape(2 * BLOCK, HEADS, VDIM)
        rope_block = lax.dynamic_slice_in_dim(rope_ext, begin, 2 * BLOCK, 0).astype(jnp.float32)
        scores = jnp.einsum('qhd,khd->hqk', query_block[:, :, :NOPE], key_block)
        scores = (scores + jnp.einsum('qhd,kd->hqk', query_block[:, :, NOPE:], rope_block)) * score_scale
        query_pos = begin + jnp.arange(BLOCK, dtype=jnp.int32)
        key_position = begin - BLOCK + jnp.arange(2 * BLOCK, dtype=jnp.int32)
        first_block = lax.dynamic_slice_in_dim(first_key, begin, BLOCK, 0)
        allowed = (key_position[None, :] >= first_block[:, None]) & (key_position[None, :] <= query_pos[:, None])
        scores = jnp.where(allowed[None, :, :], scores, -jnp.inf)
        row_max = lax.optimization_barrier(jnp.max(scores, axis=2, keepdims=True))
        exp_scores = jnp.exp(scores - row_max)
        weights = (exp_scores / lax.optimization_barrier(jnp.sum(exp_scores, axis=2, keepdims=True))).astype(jnp.bfloat16)
        result = jnp.einsum('hqk,khd->qhd', weights.astype(jnp.float32), value_block)
        return result.astype(jnp.bfloat16).reshape(BLOCK, HEADS * VDIM)
    blocks = lax.map(one_block, jnp.arange(TOKENS // BLOCK, dtype=jnp.int32))
    return blocks.reshape(TOKENS, HEADS * VDIM)
```

```python
import functools
import math

import jax
import jax.numpy as jnp
from jax import lax
from jax.experimental import pallas as pl
from jax.experimental.pallas import tpu as pltpu
from jax.sharding import PartitionSpec as P

LATENT = 512
ROPE = 64
NOPE = 128
VDIM = 128
HEAD = NOPE + ROPE
PAIR = 2 * HEAD
TILE = 256
CODE = 64
FAR = -(2.0**40)
MIB = 1 << 20


def passed_along(block, axis, distance):
    devices = range(lax.axis_size(axis))
    route = [(i - distance, i) for i in devices if i - distance in devices]
    return lax.ppermute(block, axis, route)


def doc_codes(doc_lengths, first, rows):
    position = first + jnp.arange(rows, dtype=jnp.int32)
    ends = jnp.cumsum(doc_lengths)
    doc = jnp.sum((ends[None, :] <= position[:, None]).astype(jnp.int32), axis=1)
    high, low = doc // 8, doc % 8
    lane = jnp.arange(CODE, dtype=jnp.int32)[None, :]
    hot = (lane == high[:, None]) | (lane == 32 + low[:, None])
    used = (lane < 16) | ((lane >= 32) & (lane < 40))
    inside = (position >= 0)[:, None]
    query_code = jnp.where(hot, 1.0, 0.0).astype(jnp.bfloat16)
    key_code = jnp.where(used & ~(hot & inside), FAR, 0.0).astype(jnp.bfloat16)
    return query_code, key_code


def lift_kernel(latent_ref, side_ref, key_up_ref, value_up_ref, *rest):
    key_ref, value_ref = rest[-2:]
    compact = latent_ref[:, :LATENT]
    keys = jnp.dot(compact, key_up_ref[...], preferred_element_type=jnp.float32).astype(jnp.bfloat16)
    values = jnp.dot(compact, value_up_ref[...], preferred_element_type=jnp.float32)
    value_ref[...] = values.astype(jnp.bfloat16)
    rope_code, code_rope = side_ref[:, :128], side_ref[:, 128:]
    left = lax.broadcasted_iota(jnp.int32, rope_code.shape, 1) < CODE
    for head in range(keys.shape[1] // (2 * NOPE)):
        at = head * 2 * NOPE
        first, second = keys[:, at : at + NOPE], keys[:, at + NOPE : at + 2 * NOPE]
        if head % 2 == 0:
            second = rope_code
        else:
            first = jnp.where(left, code_rope, first)
            second = jnp.where(left, second, code_rope)
        key_ref[:, at : at + NOPE] = first
        key_ref[:, at + NOPE : at + 2 * NOPE] = second


def lift(latent_rows, side, key_up, value_up, total_rows, first_row, held=None):
    rows = latent_rows.shape[0]
    key_cols, value_cols = key_up.shape[1], value_up.shape[1]
    first_step = first_row // TILE
    whole = lambda a: pl.BlockSpec(a.shape, lambda i: (0, 0))
    operands = [latent_rows, side, key_up, value_up]
    in_specs = [
        pl.BlockSpec((TILE, latent_rows.shape[1]), lambda i: (i, 0)),
        pl.BlockSpec((TILE, side.shape[1]), lambda i: (i, 0)),
        whole(key_up),
        whole(value_up),
    ]
    aliases = {}
    if held is not None:
        operands += list(held)
        in_specs += [pl.BlockSpec(memory_space=pl.ANY)] * 2
        aliases = {4: 0, 5: 1}
    return pl.pallas_call(
        lift_kernel,
        grid=(rows // TILE,),
        in_specs=in_specs,
        out_specs=[
            pl.BlockSpec((TILE, key_cols), lambda i: (first_step + i, 0)),
            pl.BlockSpec((TILE, value_cols), lambda i: (first_step + i, 0)),
        ],
        out_shape=[
            jax.ShapeDtypeStruct((total_rows, key_cols), jnp.bfloat16),
            jax.ShapeDtypeStruct((total_rows, value_cols), jnp.bfloat16),
        ],
        input_output_aliases=aliases,
        compiler_params=pltpu.CompilerParams(vmem_limit_bytes=16 * MIB),
        cost_estimate=pl.CostEstimate(
            flops=2 * rows * LATENT * (key_cols + value_cols),
            bytes_accessed=2 * rows * (key_cols + value_cols + 768),
            transcendentals=0,
        ),
        name="lift",
    )(*operands)


def attend_kernel(window, query_ref, code_ref, key_ref, value_ref, out_ref):
    to_log2 = math.log2(math.e) / math.sqrt(HEAD)
    left = lax.broadcasted_iota(jnp.int32, (TILE, 128), 1) < CODE
    causal = lax.broadcasted_iota(jnp.int32, (TILE, TILE), 1) <= lax.broadcasted_iota(
        jnp.int32, (TILE, TILE), 0
    )
    ones = jnp.ones((window, 128), jnp.bfloat16)

    @pl.loop(0, query_ref.shape[0] // TILE)
    def _(step):
        begin = pl.multiple_of(step * TILE, TILE)
        rows = pl.ds(begin, TILE)
        span = pl.ds(begin, window)
        code = code_ref[rows, :]
        for head in range(2):
            if head == 0:
                query = jnp.concatenate(
                    [query_ref[rows, :128], jnp.where(left, query_ref[rows, 128:256], code)], axis=1
                )
            else:
                query = jnp.concatenate(
                    [jnp.where(left, code, query_ref[rows, 128:256]), query_ref[rows, 256:384]], axis=1
                )
            keys = key_ref[span, head * 256 : (head + 1) * 256]
            scores = lax.dot_general(
                query, keys, (((1,), (1,)), ((), ())), preferred_element_type=jnp.float32
            )
            own = jnp.where(causal, scores[:, window - TILE :], FAR)
            scores = jnp.concatenate([scores[:, : window - TILE], own], axis=1)
            top = jnp.max(scores, axis=1, keepdims=True) * to_log2
            weights = jnp.exp2(scores * to_log2 - top).astype(jnp.bfloat16)
            values = jnp.concatenate(
                [value_ref[span, head * VDIM : (head + 1) * VDIM], ones], axis=1
            )
            total = jnp.dot(weights, values, preferred_element_type=jnp.float32)
            result = total[:, :VDIM] / total[:, VDIM:]
            out_ref[rows, head * VDIM : (head + 1) * VDIM] = result.astype(jnp.bfloat16)


def attend(query, code, keys, values):
    rows, total = query.shape[0], keys.shape[0]
    pairs = query.shape[1] // PAIR
    window = total - rows + TILE
    return pl.pallas_call(
        functools.partial(attend_kernel, window),
        grid=(pairs,),
        in_specs=[
            pl.BlockSpec((rows, PAIR), lambda i: (0, i)),
            pl.BlockSpec(code.shape, lambda i: (0, 0)),
            pl.BlockSpec((total, 4 * NOPE), lambda i: (0, i)),
            pl.BlockSpec((total, 2 * VDIM), lambda i: (0, i)),
        ],
        out_specs=pl.BlockSpec((rows, 2 * VDIM), lambda i: (0, i)),
        out_shape=jax.ShapeDtypeStruct((rows, pairs * 2 * VDIM), jnp.bfloat16),
        compiler_params=pltpu.CompilerParams(vmem_limit_bytes=40 * MIB),
        cost_estimate=pl.CostEstimate(
            flops=4 * rows * window * pairs * 512,
            bytes_accessed=2 * (total * pairs * 768 + rows * pairs * 640),
            transcendentals=2 * pairs * rows * window,
        ),
        name="attend",
    )(query, code, keys, values)


def per_device(queries, latent, key_up, value_up, doc_lengths):
    uly_count = lax.axis_size("uly")
    own_rows = queries.shape[0]
    block_rows = own_rows * uly_count
    heads_dev = key_up.shape[1] // NOPE
    block_start = lax.axis_index("ctx") * block_rows
    pads = [(0, NOPE) if head % 2 == 0 else (CODE, ROPE) for head in range(heads_dev)]
    wide_up = jnp.concatenate(
        [jnp.pad(key_up[:, h * NOPE : (h + 1) * NOPE], ((0, 0), pads[h])) for h in range(heads_dev)],
        axis=1,
    )
    query_code, key_code = doc_codes(doc_lengths, block_start - block_rows, 2 * block_rows)
    query_code = query_code[block_rows:]
    both_codes = jnp.concatenate([query_code, query_code], axis=1)

    copies = jnp.broadcast_to(latent[None], (uly_count,) + latent.shape)
    own = lax.all_to_all(copies, "uly", split_axis=0, concat_axis=0)
    own = own.reshape(block_rows, latent.shape[1])
    previous = passed_along(own, "ctx", 1)
    local_query = lax.all_to_all(queries, "uly", split_axis=1, concat_axis=0, tiled=True)

    def side_of(rows, code):
        rope = rows[:, LATENT:]
        return jnp.concatenate([rope, code, code, rope], axis=1)

    held = lift(own, side_of(own, key_code[block_rows:]), wide_up, value_up, 2 * block_rows, block_rows)
    keys, values = lift(
        previous, side_of(previous, key_code[:block_rows]), wide_up, value_up, 2 * block_rows, 0, held
    )
    result = attend(local_query, both_codes, keys, values)
    result = result.reshape(uly_count, own_rows, heads_dev * VDIM)
    result = lax.all_to_all(result, "uly", split_axis=0, concat_axis=0)
    return jnp.transpose(result, (1, 0, 2)).reshape(own_rows, uly_count * heads_dev * VDIM)


def solution(mesh):
    placed = (P(("ctx", "uly"), None), P(("ctx", "uly"), None), P(None, "uly"), P(None, "uly"), P())
    return jax.shard_map(
        per_device, mesh=mesh, in_specs=placed, out_specs=P(("ctx", "uly"), None), check_vma=False
    )
```

```python
import functools
import math

import jax
import jax.numpy as jnp
from jax import lax
from jax.experimental import pallas as pl
from jax.experimental.pallas import tpu as pltpu
from jax.sharding import PartitionSpec as P

LATENT = 512
ROPE = 64
NOPE = 128
VDIM = 128
HEAD = NOPE + ROPE
PAIR = 2 * HEAD
WIDE = LATENT + 2 * ROPE
TILE = 256
CODE = 64
FAR = -(2.0**40)
MIB = 1 << 20


def passed_along(block, axis, distance):
    devices = range(lax.axis_size(axis))
    route = [(i - distance, i) for i in devices if i - distance in devices]
    return lax.ppermute(block, axis, route)


def doc_codes(doc_lengths, first, rows):
    position = first + jnp.arange(rows, dtype=jnp.int32)
    ends = jnp.cumsum(doc_lengths)
    doc = jnp.sum((ends[None, :] <= position[:, None]).astype(jnp.int32), axis=1)
    high, low = doc // 8, doc % 8
    lane = (jnp.arange(2 * CODE, dtype=jnp.int32) % CODE)[None, :]
    hot = (lane == high[:, None]) | (lane == 32 + low[:, None])
    used = (lane < 16) | ((lane >= 32) & (lane < 40))
    inside = (position >= 0)[:, None]
    query_code = jnp.where(hot, 1.0, 0.0).astype(jnp.bfloat16)
    key_code = jnp.where(used & ~(hot & inside), FAR, 0.0).astype(jnp.bfloat16)
    return query_code, key_code


def first_tiles(doc_lengths, block_start, block_rows):
    starts = jnp.cumsum(doc_lengths) - doc_lengths
    position = block_start + TILE * jnp.arange(block_rows // TILE, dtype=jnp.int32)
    before = starts[None, :] <= position[:, None]
    first_key = jnp.max(jnp.where(before, starts[None, :], 0), axis=1)
    return (first_key - (block_start - block_rows)) // TILE


def spread_kernel(latent_ref, copies_ref, wide, sems):
    wide[:, :LATENT] = latent_ref[:, :LATENT]
    rope = latent_ref[:, LATENT:]
    wide[:, LATENT:] = jnp.concatenate([rope, rope], axis=1)
    copies = [
        pltpu.make_async_copy(wide, copies_ref.at[i], sems.at[i]) for i in range(copies_ref.shape[0])
    ]
    for copy in copies:
        copy.start()
    for copy in copies:
        copy.wait()


def spread(latent, count):
    rows = latent.shape[0]
    return pl.pallas_call(
        spread_kernel,
        in_specs=[pl.BlockSpec(memory_space=pltpu.VMEM)],
        out_specs=pl.BlockSpec(memory_space=pl.ANY),
        out_shape=jax.ShapeDtypeStruct((count, rows, WIDE), latent.dtype),
        scratch_shapes=[pltpu.VMEM((rows, WIDE), latent.dtype), pltpu.SemaphoreType.DMA((count,))],
        compiler_params=pltpu.CompilerParams(vmem_limit_bytes=60 * MIB),
        name="spread",
    )(latent)


def lift_kernel(latent_ref, code_ref, key_up_ref, value_up_ref, key_ref, value_ref):
    compact = latent_ref[:, :LATENT]
    keys = jnp.dot(compact, key_up_ref[...], preferred_element_type=jnp.float32).astype(jnp.bfloat16)
    values = jnp.dot(compact, value_up_ref[...], preferred_element_type=jnp.float32)
    value_ref[...] = values.astype(jnp.bfloat16)
    rope, code = latent_ref[:, LATENT:], code_ref[...]
    left = lax.broadcasted_iota(jnp.int32, rope.shape, 1) < CODE
    for head in range(keys.shape[1] // (2 * NOPE)):
        at = head * 2 * NOPE
        first, second = keys[:, at : at + NOPE], keys[:, at + NOPE : at + 2 * NOPE]
        if head % 2 == 0:
            second = jnp.where(left, rope, code)
        else:
            first = jnp.where(left, code, first)
            second = jnp.where(left, second, rope)
        key_ref[:, at : at + NOPE] = first
        key_ref[:, at + NOPE : at + 2 * NOPE] = second


def lift(latent_rows, code, key_up, value_up):
    rows = latent_rows.shape[0]
    key_cols, value_cols = key_up.shape[1], value_up.shape[1]
    tiled = lambda cols: pl.BlockSpec((TILE, cols), lambda i: (i, 0))
    whole = lambda a: pl.BlockSpec(a.shape, lambda i: (0, 0))
    return pl.pallas_call(
        lift_kernel,
        grid=(rows // TILE,),
        in_specs=[tiled(WIDE), tiled(2 * CODE), whole(key_up), whole(value_up)],
        out_specs=[tiled(key_cols), tiled(value_cols)],
        out_shape=[
            jax.ShapeDtypeStruct((rows, key_cols), jnp.bfloat16),
            jax.ShapeDtypeStruct((rows, value_cols), jnp.bfloat16),
        ],
        compiler_params=pltpu.CompilerParams(vmem_limit_bytes=60 * MIB),
        cost_estimate=pl.CostEstimate(
            flops=2 * rows * LATENT * (key_cols + value_cols),
            bytes_accessed=2 * rows * (key_cols + value_cols + 768),
            transcendentals=0,
        ),
        name="lift",
    )(latent_rows, code, key_up, value_up)


def attend_kernel(
    first_ref, query_hbm, code_ref, key_prev, value_prev, key_own, value_own, out_hbm,
    query_ref, key_ref, value_ref, out_ref, key_sems, value_sems, query_sems, out_sems,
):
    tiles = query_ref.shape[0] // TILE
    heads = value_ref.shape[1] // VDIM
    to_log2 = math.log2(math.e) / math.sqrt(HEAD)
    first_tile = first_ref[0]

    def tile_rows(tile):
        return pl.ds(pl.multiple_of(tile * TILE, TILE), TILE)

    def key_copies(tile):
        here = tile_rows(tile)
        if tile < tiles:
            sources = (key_prev.at[here], value_prev.at[here])
        else:
            there = tile_rows(tile - tiles)
            sources = (key_own.at[there], value_own.at[there])
        return (
            pltpu.make_async_copy(sources[0], key_ref.at[here], key_sems.at[tile]),
            pltpu.make_async_copy(sources[1], value_ref.at[here], value_sems.at[tile]),
        )

    def query_copy(tile):
        here = tile_rows(tile)
        return pltpu.make_async_copy(query_hbm.at[here], query_ref.at[here], query_sems.at[tile])

    def out_copy(tile):
        here = tile_rows(tile)
        return pltpu.make_async_copy(out_ref.at[here], out_hbm.at[here], out_sems.at[tile])

    def start_keys(tile):
        for copy in key_copies(tile):
            copy.start()

    def wait_keys(tile):
        for copy in key_copies(tile):
            copy.wait()

    query_copy(0).start()
    start_keys(tiles)
    for tile in reversed(range(tiles)):
        pl.when(first_tile <= tile)(functools.partial(start_keys, tile))
    for tile in range(1, tiles):
        query_copy(tile).start()
        start_keys(tiles + tile)

    left = lax.broadcasted_iota(jnp.int32, (TILE, 128), 1) < CODE
    causal = lax.broadcasted_iota(jnp.int32, (TILE, TILE), 1) <= lax.broadcasted_iota(
        jnp.int32, (TILE, TILE), 0
    )

    def score(head, rows, span, code):
        at = head // 2 * PAIR
        middle = query_ref[rows, at + 128 : at + 256]
        if head % 2 == 0:
            query = [query_ref[rows, at : at + 128], jnp.where(left, middle, code)]
        else:
            query = [jnp.where(left, code, middle), query_ref[rows, at + 256 : at + 384]]
        return lax.dot_general(
            jnp.concatenate(query, axis=1),
            key_ref[span, head * 256 : (head + 1) * 256],
            (((1,), (1,)), ((), ())),
            preferred_element_type=jnp.float32,
        )

    def weigh(scores):
        far = scores.shape[1] - TILE
        own = jnp.where(causal, scores[:, far:], FAR)
        scores = jnp.concatenate([scores[:, :far], own], axis=1) if far else own
        top = jnp.max(scores, axis=1, keepdims=True) * to_log2
        return jnp.exp2(scores * to_log2 - top).astype(jnp.bfloat16)

    def attend_rows(step, count):
        rows = tile_rows(step)
        span = pl.ds(pl.multiple_of((tiles + 1 + step - count) * TILE, TILE), count * TILE)
        code = code_ref[rows, :]
        scores = [score(head, rows, span, code) for head in range(heads)]
        weights = [weigh(s) for s in scores]
        for head in range(heads):
            cols = slice(head * VDIM, (head + 1) * VDIM)
            ones = jnp.ones((count * TILE, VDIM), jnp.bfloat16)
            values = jnp.concatenate([value_ref[span, cols], ones], axis=1)
            total = jnp.dot(weights[head], values, preferred_element_type=jnp.float32)
            out_ref[rows, cols] = (total[:, :VDIM] / total[:, VDIM:]).astype(jnp.bfloat16)

    @pl.loop(0, tiles)
    def _(step):
        @pl.when(step == 0)
        def _():
            for tile in reversed(range(tiles)):
                pl.when(first_tile <= tile)(functools.partial(wait_keys, tile))

        for tile in range(tiles):

            @pl.when(step == tile)
            def _():
                query_copy(tile).wait()
                wait_keys(tiles + tile)

        count = tiles + 1 + step - first_ref[step]
        for n in range(1, tiles + 2):
            pl.when(count == n)(functools.partial(attend_rows, step, n))
        out_copy(step).start()

    for tile in range(tiles):
        out_copy(tile).wait()


def attend(first, query, code, key_prev, value_prev, key_own, value_own):
    rows, key_cols = key_own.shape
    value_cols = value_own.shape[1]
    tiles = rows // TILE
    vmem = pl.BlockSpec(memory_space=pltpu.VMEM)
    there = pl.BlockSpec(memory_space=pl.ANY)
    scratch = lambda r, c: pltpu.VMEM((r, c), jnp.bfloat16)
    return pl.pallas_call(
        attend_kernel,
        in_specs=[pl.BlockSpec(memory_space=pltpu.SMEM), there, vmem, there, there, there, there],
        out_specs=there,
        out_shape=jax.ShapeDtypeStruct((rows, value_cols), jnp.bfloat16),
        scratch_shapes=[
            scratch(rows, query.shape[1]),
            scratch(2 * rows, key_cols),
            scratch(2 * rows, value_cols),
            scratch(rows, value_cols),
            pltpu.SemaphoreType.DMA((2 * tiles,)),
            pltpu.SemaphoreType.DMA((2 * tiles,)),
            pltpu.SemaphoreType.DMA((tiles,)),
            pltpu.SemaphoreType.DMA((tiles,)),
        ],
        compiler_params=pltpu.CompilerParams(vmem_limit_bytes=60 * MIB),
        cost_estimate=pl.CostEstimate(
            flops=8 * rows * rows * key_cols,
            bytes_accessed=2 * rows * (2 * key_cols + 4 * value_cols),
            transcendentals=rows * rows * 4,
        ),
        name="attend",
    )(first, query, code, key_prev, value_prev, key_own, value_own)


def per_device(queries, latent, key_up, value_up, doc_lengths):
    uly_count = lax.axis_size("uly")
    own_rows = queries.shape[0]
    block_rows = own_rows * uly_count
    heads_dev = key_up.shape[1] // NOPE
    block_start = lax.axis_index("ctx") * block_rows
    pads = [(0, NOPE) if head % 2 == 0 else (CODE, ROPE) for head in range(heads_dev)]
    wide_up = jnp.concatenate(
        [jnp.pad(key_up[:, h * NOPE : (h + 1) * NOPE], ((0, 0), pads[h])) for h in range(heads_dev)],
        axis=1,
    )
    query_code, key_code = doc_codes(doc_lengths, block_start - block_rows, 2 * block_rows)
    first = first_tiles(doc_lengths, block_start, block_rows)

    own = lax.all_to_all(spread(latent, uly_count), "uly", split_axis=0, concat_axis=0)
    own = own.reshape(block_rows, WIDE)
    previous = passed_along(own, "ctx", 1)
    local_query = lax.all_to_all(queries, "uly", split_axis=1, concat_axis=0, tiled=True)
    key_own, value_own = lift(own, key_code[block_rows:], wide_up, value_up)
    key_prev, value_prev = lift(previous, key_code[:block_rows], wide_up, value_up)
    result = attend(
        first, local_query, query_code[block_rows:], key_prev, value_prev, key_own, value_own
    )
    result = result.reshape(uly_count, own_rows, heads_dev * VDIM)
    result = lax.all_to_all(result, "uly", split_axis=0, concat_axis=0)
    return jnp.transpose(result, (1, 0, 2)).reshape(own_rows, uly_count * heads_dev * VDIM)


def solution(mesh):
    placed = (P(("ctx", "uly"), None), P(("ctx", "uly"), None), P(None, "uly"), P(None, "uly"), P())
    return jax.shard_map(
        per_device, mesh=mesh, in_specs=placed, out_specs=P(("ctx", "uly"), None), check_vma=False
    )
```

```python
import functools
import math

import jax
import jax.numpy as jnp
from jax import lax
from jax.experimental import pallas as pl
from jax.experimental.pallas import tpu as pltpu
from jax.sharding import PartitionSpec as P

LATENT = 512
ROPE = 64
NOPE = 128
VDIM = 128
HEAD = NOPE + ROPE
PAIR = 2 * HEAD
CHUNKS = LATENT // 128
TILE = 256
CODE = 64
FAR = -(2.0**40)
MIB = 1 << 20


def passed_along(block, axis, distance):
    devices = range(lax.axis_size(axis))
    route = [(i - distance, i) for i in devices if i - distance in devices]
    return lax.ppermute(block, axis, route)


def doc_codes(doc_lengths, first, rows):
    position = first + jnp.arange(rows, dtype=jnp.int32)
    ends = jnp.cumsum(doc_lengths)
    doc = jnp.sum((ends[None, :] <= position[:, None]).astype(jnp.int32), axis=1)
    high, low = doc // 8, doc % 8
    lane = (jnp.arange(2 * CODE, dtype=jnp.int32) % CODE)[None, :]
    hot = (lane == high[:, None]) | (lane == 32 + low[:, None])
    used = (lane < 16) | ((lane >= 32) & (lane < 40))
    inside = (position >= 0)[:, None]
    query_code = jnp.where(hot, 1.0, 0.0).astype(jnp.bfloat16)
    key_code = jnp.where(used & ~(hot & inside), FAR, 0.0).astype(jnp.bfloat16)
    return query_code, key_code


def first_tiles(doc_lengths, block_start, block_rows):
    starts = jnp.cumsum(doc_lengths) - doc_lengths
    position = block_start + TILE * jnp.arange(block_rows // TILE, dtype=jnp.int32)
    before = starts[None, :] <= position[:, None]
    first_key = jnp.max(jnp.where(before, starts[None, :], 0), axis=1)
    return (first_key - (block_start - block_rows)) // TILE


def spread_kernel(latent_ref, copies_ref):
    rows = latent_ref.shape[0]
    half = rows // 2
    rope = latent_ref[:, LATENT:]
    chunks = [latent_ref[:, i * 128 : (i + 1) * 128] for i in range(CHUNKS)]
    packed = jnp.concatenate(chunks + [jnp.concatenate([rope[:half], rope[half:]], axis=1)], axis=0)
    for i in range(copies_ref.shape[0]):
        copies_ref[i] = packed


def spread(latent, count):
    rows = latent.shape[0]
    vmem = pl.BlockSpec(memory_space=pltpu.VMEM)
    return pl.pallas_call(
        spread_kernel,
        in_specs=[vmem],
        out_specs=vmem,
        out_shape=jax.ShapeDtypeStruct((count, rows * CHUNKS + rows // 2, 128), latent.dtype),
        compiler_params=pltpu.CompilerParams(vmem_limit_bytes=16 * MIB),
        name="spread",
    )(latent)


def lift_tile(packed, code, key_up, value_up):
    count, rows = packed.shape[0], packed.shape[1] * 2 // (2 * CHUNKS + 1)
    chunks = [
        packed[:, i * rows : (i + 1) * rows].reshape(count * rows, 128) for i in range(CHUNKS)
    ]
    compact = jnp.concatenate(chunks, axis=1)
    ropes = packed[:, CHUNKS * rows :].reshape(count * rows // 2, 128)
    low = lax.broadcasted_iota(jnp.int32, ropes.shape, 1) < ROPE
    other = jnp.concatenate([ropes[:, ROPE:], ropes[:, :ROPE]], axis=1)
    firsts = jnp.where(low, ropes, other).reshape(count, rows // 2, 128)
    seconds = jnp.where(low, other, ropes).reshape(count, rows // 2, 128)
    rope = jnp.concatenate([firsts, seconds], axis=1).reshape(count * rows, 128)
    keys = jnp.dot(compact, key_up, preferred_element_type=jnp.float32).astype(jnp.bfloat16)
    values = jnp.dot(compact, value_up, preferred_element_type=jnp.float32).astype(jnp.bfloat16)
    left = lax.broadcasted_iota(jnp.int32, rope.shape, 1) < CODE
    columns = []
    for head in range(keys.shape[1] // NOPE):
        key = keys[:, head * NOPE : (head + 1) * NOPE]
        if head % 2 == 0:
            columns += [key, jnp.where(left, rope, code)]
        else:
            turned = jnp.concatenate([key[:, CODE:], key[:, :CODE]], axis=1)
            columns += [jnp.where(left, code, turned), jnp.where(left, turned, rope)]
    return columns, values


def lift_kernel(packed_ref, code_ref, key_up_ref, value_up_ref, key_ref, value_ref):
    columns, values = lift_tile(packed_ref[...], code_ref[...], key_up_ref[...], value_up_ref[...])
    for i, column in enumerate(columns):
        key_ref[:, i * 128 : (i + 1) * 128] = column
    value_ref[...] = values


def lift(packed, code, key_up, value_up):
    rows = code.shape[0]
    steps = rows // TILE
    key_cols, value_cols = 2 * key_up.shape[1], value_up.shape[1]
    tiled = lambda cols: pl.BlockSpec((TILE, cols), lambda i: (i, 0))
    whole = lambda a: pl.BlockSpec(a.shape, lambda i: (0, 0))
    packed_spec = pl.BlockSpec((packed.shape[0] // steps,) + packed.shape[1:], lambda i: (i, 0, 0))
    return pl.pallas_call(
        lift_kernel,
        grid=(steps,),
        in_specs=[packed_spec, tiled(2 * CODE), whole(key_up), whole(value_up)],
        out_specs=[tiled(key_cols), tiled(value_cols)],
        out_shape=[
            jax.ShapeDtypeStruct((rows, key_cols), jnp.bfloat16),
            jax.ShapeDtypeStruct((rows, value_cols), jnp.bfloat16),
        ],
        compiler_params=pltpu.CompilerParams(vmem_limit_bytes=60 * MIB),
        cost_estimate=pl.CostEstimate(
            flops=2 * rows * LATENT * (key_cols + value_cols),
            bytes_accessed=2 * rows * (key_cols + value_cols + 768),
            transcendentals=0,
        ),
        name="lift",
    )(packed, code, key_up, value_up)


def attend_kernel(
    first_ref, query_hbm, code_hbm, prev_hbm, prev_code_hbm, key_up_hbm, value_up_hbm, key_own,
    value_own, out_hbm, query_ref, code_ref, prev_ref, prev_code_ref, key_up_ref, value_up_ref,
    key_ref, value_ref, out_ref, key_sems, value_sems, query_sems, out_sems, lift_sems, prev_sems,
    code_sem,
):
    tiles = query_ref.shape[0] // TILE
    heads = value_ref.shape[1] // VDIM
    to_log2 = math.log2(math.e) / math.sqrt(HEAD)
    first_tile = first_ref[0]

    def tile_rows(tile):
        return pl.ds(pl.multiple_of(tile * TILE, TILE), TILE)

    def key_copies(tile):
        here, there = tile_rows(tile), tile_rows(tiles + tile)
        return (
            pltpu.make_async_copy(key_own.at[here], key_ref.at[there], key_sems.at[tile]),
            pltpu.make_async_copy(value_own.at[here], value_ref.at[there], value_sems.at[tile]),
        )

    def query_copy(tile):
        here = tile_rows(tile)
        return pltpu.make_async_copy(query_hbm.at[here], query_ref.at[here], query_sems.at[tile])

    def out_copy(tile):
        here = tile_rows(tile)
        return pltpu.make_async_copy(out_ref.at[here], out_hbm.at[here], out_sems.at[tile])

    share = prev_ref.shape[0] // tiles

    def prev_copy(tile):
        here = pl.ds(tile * share, share)
        return pltpu.make_async_copy(prev_hbm.at[here], prev_ref.at[here], prev_sems.at[tile])

    lift_copies = [
        pltpu.make_async_copy(source, target, lift_sems.at[i])
        for i, (source, target) in enumerate(
            [(key_up_hbm, key_up_ref), (value_up_hbm, value_up_ref), (prev_code_hbm, prev_code_ref)]
        )
    ]
    code_copy = pltpu.make_async_copy(code_hbm, code_ref, code_sem)

    @pl.when(first_tile < tiles)
    def _():
        for copy in lift_copies:
            copy.start()
        for tile in range(tiles):
            pl.when(first_tile <= tile)(lambda tile=tile: prev_copy(tile).start())

    code_copy.start()
    for tile in range(tiles):
        query_copy(tile).start()
        for copy in key_copies(tile):
            copy.start()

    @pl.when(first_tile < tiles)
    def _():
        for copy in lift_copies:
            copy.wait()

    @pl.loop(jnp.minimum(first_tile, tiles), tiles)
    def _(tile):
        prev_copy(tile).wait()
        rows = tile_rows(tile)
        packed = prev_ref[pl.ds(tile * share, share)]
        columns, values = lift_tile(packed, prev_code_ref[rows, :], key_up_ref[...], value_up_ref[...])
        for i, column in enumerate(columns):
            key_ref[rows, i * 128 : (i + 1) * 128] = column
        value_ref[rows, :] = values

    left = lax.broadcasted_iota(jnp.int32, (TILE, 128), 1) < CODE
    causal = lax.broadcasted_iota(jnp.int32, (TILE, TILE), 1) <= lax.broadcasted_iota(
        jnp.int32, (TILE, TILE), 0
    )

    def score(head, rows, span, code):
        at = head // 2 * PAIR
        middle = query_ref[rows, at + 128 : at + 256]
        if head % 2 == 0:
            query = [query_ref[rows, at : at + 128], jnp.where(left, middle, code)]
        else:
            query = [jnp.where(left, code, middle), query_ref[rows, at + 256 : at + 384]]
        return lax.dot_general(
            jnp.concatenate(query, axis=1),
            key_ref[span, head * 256 : (head + 1) * 256],
            (((1,), (1,)), ((), ())),
            preferred_element_type=jnp.float32,
        )

    def weigh(scores):
        far = scores.shape[1] - TILE
        own = jnp.where(causal, scores[:, far:], FAR)
        scores = jnp.concatenate([scores[:, :far], own], axis=1) if far else own
        top = jnp.max(scores, axis=1, keepdims=True) * to_log2
        return jnp.exp2(scores * to_log2 - top).astype(jnp.bfloat16)

    def attend_rows(step, count):
        rows = tile_rows(step)
        span = pl.ds(pl.multiple_of((tiles + 1 + step - count) * TILE, TILE), count * TILE)
        code = code_ref[rows, :]
        scores = [score(head, rows, span, code) for head in range(heads)]
        weights = [weigh(s) for s in scores]
        for head in range(heads):
            cols = slice(head * VDIM, (head + 1) * VDIM)
            ones = jnp.ones((count * TILE, VDIM), jnp.bfloat16)
            values = jnp.concatenate([value_ref[span, cols], ones], axis=1)
            total = jnp.dot(weights[head], values, preferred_element_type=jnp.float32)
            out_ref[rows, cols] = (total[:, :VDIM] / total[:, VDIM:]).astype(jnp.bfloat16)

    code_copy.wait()

    @pl.loop(0, tiles)
    def _(step):
        for tile in range(tiles):

            @pl.when(step == tile)
            def _():
                query_copy(tile).wait()
                for copy in key_copies(tile):
                    copy.wait()

        count = tiles + 1 + step - first_ref[step]
        for n in range(1, tiles + 2):
            pl.when(count == n)(functools.partial(attend_rows, step, n))
        out_copy(step).start()

    for tile in range(tiles):
        out_copy(tile).wait()


def attend(first, query, code, prev, prev_code, key_up, value_up, key_own, value_own):
    rows, key_cols = key_own.shape
    value_cols = value_own.shape[1]
    tiles = rows // TILE
    there = pl.BlockSpec(memory_space=pl.ANY)
    scratch = lambda *shape: pltpu.VMEM(shape, jnp.bfloat16)
    return pl.pallas_call(
        attend_kernel,
        in_specs=[pl.BlockSpec(memory_space=pltpu.SMEM)] + [there] * 8,
        out_specs=there,
        out_shape=jax.ShapeDtypeStruct((rows, value_cols), jnp.bfloat16),
        scratch_shapes=[
            scratch(*query.shape),
            scratch(*code.shape),
            scratch(*prev.shape),
            scratch(*prev_code.shape),
            scratch(*key_up.shape),
            scratch(*value_up.shape),
            scratch(2 * rows, key_cols),
            scratch(2 * rows, value_cols),
            scratch(rows, value_cols),
            pltpu.SemaphoreType.DMA((tiles,)),
            pltpu.SemaphoreType.DMA((tiles,)),
            pltpu.SemaphoreType.DMA((tiles,)),
            pltpu.SemaphoreType.DMA((tiles,)),
            pltpu.SemaphoreType.DMA((3,)),
            pltpu.SemaphoreType.DMA((tiles,)),
            pltpu.SemaphoreType.DMA,
        ],
        compiler_params=pltpu.CompilerParams(vmem_limit_bytes=60 * MIB),
        cost_estimate=pl.CostEstimate(
            flops=8 * rows * rows * key_cols,
            bytes_accessed=2 * rows * (2 * key_cols + 4 * value_cols),
            transcendentals=rows * rows * 4,
        ),
        name="attend",
    )(first, query, code, prev, prev_code, key_up, value_up, key_own, value_own)


def per_device(queries, latent, key_up, value_up, doc_lengths):
    uly_count = lax.axis_size("uly")
    own_rows = queries.shape[0]
    block_rows = own_rows * uly_count
    heads_dev = key_up.shape[1] // NOPE
    block_start = lax.axis_index("ctx") * block_rows
    query_code, key_code = doc_codes(doc_lengths, block_start - block_rows, 2 * block_rows)
    first = first_tiles(doc_lengths, block_start, block_rows)

    own = lax.all_to_all(spread(latent, uly_count), "uly", split_axis=0, concat_axis=0)
    previous = passed_along(own, "ctx", 1)
    local_query = lax.all_to_all(queries, "uly", split_axis=1, concat_axis=0, tiled=True)
    key_own, value_own = lift(own, key_code[block_rows:], key_up, value_up)
    result = attend(
        first, local_query, query_code[block_rows:], previous, key_code[:block_rows], key_up, value_up,
        key_own, value_own,
    )
    result = result.reshape(uly_count, own_rows, heads_dev * VDIM)
    result = lax.all_to_all(result, "uly", split_axis=0, concat_axis=0)
    return jnp.transpose(result, (1, 0, 2)).reshape(own_rows, uly_count * heads_dev * VDIM)


def solution(mesh):
    placed = (P(("ctx", "uly"), None), P(("ctx", "uly"), None), P(None, "uly"), P(None, "uly"), P())
    return jax.shard_map(
        per_device, mesh=mesh, in_specs=placed, out_specs=P(("ctx", "uly"), None), check_vma=False
    )
```

```python
import functools
import math

import jax
import jax.numpy as jnp
from jax import lax
from jax.experimental import pallas as pl
from jax.experimental.pallas import tpu as pltpu
from jax.sharding import PartitionSpec as P

LATENT = 512
ROPE = 64
NOPE = 128
VDIM = 128
HEAD = NOPE + ROPE
PAIR = 2 * HEAD
CHUNKS = LATENT // 128
TILE = 256
CODE = 64
FAR = -(2.0**40)
MIB = 1 << 20


def passed_along(block, axis, distance):
    devices = range(lax.axis_size(axis))
    route = [(i - distance, i) for i in devices if i - distance in devices]
    return lax.ppermute(block, axis, route)


def doc_codes(doc_lengths, first, rows):
    position = first + jnp.arange(rows, dtype=jnp.int32)
    ends = jnp.cumsum(doc_lengths)
    doc = jnp.sum((ends[None, :] <= position[:, None]).astype(jnp.int32), axis=1)
    high, low = doc // 8, doc % 8
    lane = (jnp.arange(2 * CODE, dtype=jnp.int32) % CODE)[None, :]
    hot = (lane == high[:, None]) | (lane == 32 + low[:, None])
    used = (lane < 16) | ((lane >= 32) & (lane < 40))
    inside = (position >= 0)[:, None]
    query_code = jnp.where(hot, 1.0, 0.0).astype(jnp.bfloat16)
    key_code = jnp.where(used & ~(hot & inside), FAR, 0.0).astype(jnp.bfloat16)
    return query_code, key_code


def first_tiles(doc_lengths, block_start, block_rows):
    starts = jnp.cumsum(doc_lengths) - doc_lengths
    position = block_start + TILE * jnp.arange(block_rows // TILE, dtype=jnp.int32)
    before = starts[None, :] <= position[:, None]
    first_key = jnp.max(jnp.where(before, starts[None, :], 0), axis=1)
    return (first_key - (block_start - block_rows)) // TILE


def spread_kernel(latent_ref, copies_ref):
    rows = latent_ref.shape[0]
    half = rows // 2
    rope = latent_ref[:, LATENT:]
    chunks = [latent_ref[:, i * 128 : (i + 1) * 128] for i in range(CHUNKS)]
    packed = jnp.concatenate(chunks + [jnp.concatenate([rope[:half], rope[half:]], axis=1)], axis=0)
    for i in range(copies_ref.shape[0]):
        copies_ref[i] = packed


def spread(latent, count):
    rows = latent.shape[0]
    vmem = pl.BlockSpec(memory_space=pltpu.VMEM)
    return pl.pallas_call(
        spread_kernel,
        in_specs=[vmem],
        out_specs=vmem,
        out_shape=jax.ShapeDtypeStruct((count, rows * CHUNKS + rows // 2, 128), latent.dtype),
        compiler_params=pltpu.CompilerParams(vmem_limit_bytes=16 * MIB),
        name="spread",
    )(latent)


def lift_tile(packed, code, key_up, value_up):
    count, rows = packed.shape[0], packed.shape[1] * 2 // (2 * CHUNKS + 1)
    chunks = [
        packed[:, i * rows : (i + 1) * rows].reshape(count * rows, 128) for i in range(CHUNKS)
    ]
    compact = jnp.concatenate(chunks, axis=1)
    ropes = packed[:, CHUNKS * rows :].reshape(count * rows // 2, 128)
    low = lax.broadcasted_iota(jnp.int32, ropes.shape, 1) < ROPE
    other = jnp.concatenate([ropes[:, ROPE:], ropes[:, :ROPE]], axis=1)
    firsts = jnp.where(low, ropes, other).reshape(count, rows // 2, 128)
    seconds = jnp.where(low, other, ropes).reshape(count, rows // 2, 128)
    rope = jnp.concatenate([firsts, seconds], axis=1).reshape(count * rows, 128)
    keys = jnp.dot(compact, key_up, preferred_element_type=jnp.float32).astype(jnp.bfloat16)
    values = jnp.dot(compact, value_up, preferred_element_type=jnp.float32).astype(jnp.bfloat16)
    left = lax.broadcasted_iota(jnp.int32, rope.shape, 1) < CODE
    columns = []
    for head in range(keys.shape[1] // NOPE):
        key = keys[:, head * NOPE : (head + 1) * NOPE]
        if head % 2 == 0:
            columns += [key, jnp.where(left, rope, code)]
        else:
            turned = jnp.concatenate([key[:, CODE:], key[:, :CODE]], axis=1)
            columns += [jnp.where(left, code, turned), jnp.where(left, turned, rope)]
    return columns, values


def lift_kernel(packed_ref, code_ref, key_up_ref, value_up_ref, rows_ref):
    columns, values = lift_tile(packed_ref[...], code_ref[...], key_up_ref[...], value_up_ref[...])
    for i, column in enumerate(columns):
        rows_ref[:, i * 128 : (i + 1) * 128] = column
    rows_ref[:, len(columns) * 128 :] = values


def lift(packed, code, key_up, value_up):
    rows = code.shape[0]
    steps = rows // TILE
    key_cols, value_cols = 2 * key_up.shape[1], value_up.shape[1]
    tiled = lambda cols: pl.BlockSpec((TILE, cols), lambda i: (i, 0))
    whole = lambda a: pl.BlockSpec(a.shape, lambda i: (0, 0))
    packed_spec = pl.BlockSpec((packed.shape[0] // steps,) + packed.shape[1:], lambda i: (i, 0, 0))
    return pl.pallas_call(
        lift_kernel,
        grid=(steps,),
        in_specs=[packed_spec, tiled(2 * CODE), whole(key_up), whole(value_up)],
        out_specs=tiled(key_cols + value_cols),
        out_shape=jax.ShapeDtypeStruct((rows, key_cols + value_cols), jnp.bfloat16),
        compiler_params=pltpu.CompilerParams(vmem_limit_bytes=60 * MIB),
        cost_estimate=pl.CostEstimate(
            flops=2 * rows * LATENT * (key_cols + value_cols),
            bytes_accessed=2 * rows * (key_cols + value_cols + 768),
            transcendentals=0,
        ),
        name="lift",
    )(packed, code, key_up, value_up)


def attend_kernel(
    first_ref, query_hbm, code_hbm, prev_hbm, prev_code_hbm, key_up_hbm, value_up_hbm, own_hbm,
    out_hbm, query_ref, code_ref, prev_ref, prev_code_ref, key_up_ref, value_up_ref,
    key_ref, value_ref, out_ref, key_sems, value_sems, query_sems, out_sems, lift_sems, prev_sems,
    code_sem,
):
    tiles = query_ref.shape[0] // TILE
    heads = value_ref.shape[1] // VDIM
    key_cols = key_ref.shape[1]
    to_log2 = math.log2(math.e) / math.sqrt(HEAD)
    first_tile = first_ref[0]

    def tile_rows(tile):
        return pl.ds(pl.multiple_of(tile * TILE, TILE), TILE)

    def key_copies(tile):
        here, there = tile_rows(tile), tile_rows(tiles + tile)
        return (
            pltpu.make_async_copy(
                own_hbm.at[here, :key_cols], key_ref.at[there], key_sems.at[tile]
            ),
            pltpu.make_async_copy(
                own_hbm.at[here, key_cols:], value_ref.at[there], value_sems.at[tile]
            ),
        )

    def query_copy(tile):
        here = tile_rows(tile)
        return pltpu.make_async_copy(query_hbm.at[here], query_ref.at[here], query_sems.at[tile])

    def out_copy(tile):
        here = tile_rows(tile)
        return pltpu.make_async_copy(out_ref.at[here], out_hbm.at[here], out_sems.at[tile])

    share = prev_ref.shape[0] // tiles

    def prev_copy(tile):
        here = pl.ds(tile * share, share)
        return pltpu.make_async_copy(prev_hbm.at[here], prev_ref.at[here], prev_sems.at[tile])

    lift_copies = [
        pltpu.make_async_copy(source, target, lift_sems.at[i])
        for i, (source, target) in enumerate(
            [(key_up_hbm, key_up_ref), (value_up_hbm, value_up_ref), (prev_code_hbm, prev_code_ref)]
        )
    ]
    code_copy = pltpu.make_async_copy(code_hbm, code_ref, code_sem)

    @pl.when(first_tile < tiles)
    def _():
        for copy in lift_copies:
            copy.start()
        for tile in range(tiles):
            pl.when(first_tile <= tile)(lambda tile=tile: prev_copy(tile).start())

    code_copy.start()
    for tile in range(tiles):
        query_copy(tile).start()
        for copy in key_copies(tile):
            copy.start()

    @pl.when(first_tile < tiles)
    def _():
        for copy in lift_copies:
            copy.wait()

    @pl.loop(jnp.minimum(first_tile, tiles), tiles)
    def _(tile):
        prev_copy(tile).wait()
        rows = tile_rows(tile)
        packed = prev_ref[pl.ds(tile * share, share)]
        columns, values = lift_tile(packed, prev_code_ref[rows, :], key_up_ref[...], value_up_ref[...])
        for i, column in enumerate(columns):
            key_ref[rows, i * 128 : (i + 1) * 128] = column
        value_ref[rows, :] = values

    left = lax.broadcasted_iota(jnp.int32, (TILE, 128), 1) < CODE
    causal = lax.broadcasted_iota(jnp.int32, (TILE, TILE), 1) <= lax.broadcasted_iota(
        jnp.int32, (TILE, TILE), 0
    )

    def score(head, rows, span, code):
        at = head // 2 * PAIR
        middle = query_ref[rows, at + 128 : at + 256]
        if head % 2 == 0:
            query = [query_ref[rows, at : at + 128], jnp.where(left, middle, code)]
        else:
            query = [jnp.where(left, code, middle), query_ref[rows, at + 256 : at + 384]]
        return lax.dot_general(
            jnp.concatenate(query, axis=1),
            key_ref[span, head * 256 : (head + 1) * 256],
            (((1,), (1,)), ((), ())),
            preferred_element_type=jnp.float32,
        )

    def weigh(scores):
        far = scores.shape[1] - TILE
        own = jnp.where(causal, scores[:, far:], FAR)
        scores = jnp.concatenate([scores[:, :far], own], axis=1) if far else own
        top = jnp.max(scores, axis=1, keepdims=True) * to_log2
        return jnp.exp2(scores * to_log2 - top).astype(jnp.bfloat16)

    def attend_rows(step, count):
        rows = tile_rows(step)
        span = pl.ds(pl.multiple_of((tiles + 1 + step - count) * TILE, TILE), count * TILE)
        code = code_ref[rows, :]
        scores = [score(head, rows, span, code) for head in range(heads)]
        weights = [weigh(s) for s in scores]
        for head in range(heads):
            cols = slice(head * VDIM, (head + 1) * VDIM)
            ones = jnp.ones((count * TILE, VDIM), jnp.bfloat16)
            values = jnp.concatenate([value_ref[span, cols], ones], axis=1)
            total = jnp.dot(weights[head], values, preferred_element_type=jnp.float32)
            out_ref[rows, cols] = (total[:, :VDIM] / total[:, VDIM:]).astype(jnp.bfloat16)

    code_copy.wait()

    @pl.loop(0, tiles)
    def _(step):
        for tile in range(tiles):

            @pl.when(step == tile)
            def _():
                query_copy(tile).wait()
                for copy in key_copies(tile):
                    copy.wait()

        count = tiles + 1 + step - first_ref[step]
        for n in range(1, tiles + 2):
            pl.when(count == n)(functools.partial(attend_rows, step, n))
        out_copy(step).start()

    for tile in range(tiles):
        out_copy(tile).wait()


def attend(first, query, code, prev, prev_code, key_up, value_up, own):
    rows, value_cols = own.shape[0], value_up.shape[1]
    key_cols = own.shape[1] - value_cols
    tiles = rows // TILE
    there = pl.BlockSpec(memory_space=pl.ANY)
    scratch = lambda *shape: pltpu.VMEM(shape, jnp.bfloat16)
    return pl.pallas_call(
        attend_kernel,
        in_specs=[pl.BlockSpec(memory_space=pltpu.SMEM)] + [there] * 7,
        out_specs=there,
        out_shape=jax.ShapeDtypeStruct((rows, value_cols), jnp.bfloat16),
        scratch_shapes=[
            scratch(*query.shape),
            scratch(*code.shape),
            scratch(*prev.shape),
            scratch(*prev_code.shape),
            scratch(*key_up.shape),
            scratch(*value_up.shape),
            scratch(2 * rows, key_cols),
            scratch(2 * rows, value_cols),
            scratch(rows, value_cols),
            pltpu.SemaphoreType.DMA((tiles,)),
            pltpu.SemaphoreType.DMA((tiles,)),
            pltpu.SemaphoreType.DMA((tiles,)),
            pltpu.SemaphoreType.DMA((tiles,)),
            pltpu.SemaphoreType.DMA((3,)),
            pltpu.SemaphoreType.DMA((tiles,)),
            pltpu.SemaphoreType.DMA,
        ],
        compiler_params=pltpu.CompilerParams(vmem_limit_bytes=50 * MIB),
        cost_estimate=pl.CostEstimate(
            flops=8 * rows * rows * key_cols,
            bytes_accessed=2 * rows * (2 * key_cols + 4 * value_cols),
            transcendentals=rows * rows * 4,
        ),
        name="attend",
    )(first, query, code, prev, prev_code, key_up, value_up, own)


def per_device(queries, latent, key_up, value_up, doc_lengths):
    uly_count = lax.axis_size("uly")
    own_rows = queries.shape[0]
    block_rows = own_rows * uly_count
    heads_dev = key_up.shape[1] // NOPE
    block_start = lax.axis_index("ctx") * block_rows
    query_code, key_code = doc_codes(doc_lengths, block_start - block_rows, 2 * block_rows)
    first = first_tiles(doc_lengths, block_start, block_rows)

    own = lax.all_to_all(spread(latent, uly_count), "uly", split_axis=0, concat_axis=0)
    previous = passed_along(own, "ctx", 1)
    local_query = lax.all_to_all(queries, "uly", split_axis=1, concat_axis=0, tiled=True)
    own_rows_lifted = lift(own, key_code[block_rows:], key_up, value_up)
    result = attend(
        first, local_query, query_code[block_rows:], previous, key_code[:block_rows], key_up, value_up,
        own_rows_lifted,
    )
    result = result.reshape(uly_count, own_rows, heads_dev * VDIM)
    result = lax.all_to_all(result, "uly", split_axis=0, concat_axis=0)
    return jnp.transpose(result, (1, 0, 2)).reshape(own_rows, uly_count * heads_dev * VDIM)


def solution(mesh):
    placed = (P(("ctx", "uly"), None), P(("ctx", "uly"), None), P(None, "uly"), P(None, "uly"), P())
    return jax.shard_map(
        per_device, mesh=mesh, in_specs=placed, out_specs=P(("ctx", "uly"), None), check_vma=False
    )
```

```python
import functools
import math

import jax
import jax.numpy as jnp
from jax import lax
from jax.experimental import pallas as pl
from jax.experimental.pallas import tpu as pltpu
from jax.sharding import PartitionSpec as P

LATENT = 512
ROPE = 64
NOPE = 128
VDIM = 128
HEAD = NOPE + ROPE
PAIR = 2 * HEAD
CHUNKS = LATENT // 128
TILE = 256
CODE = 64
FAR = -(2.0**40)
MIB = 1 << 20


def passed_along(block, axis, senders):
    last = lax.axis_size(axis) - 1
    return lax.ppermute(block, axis, [(i, i + 1) for i in senders if i < last])


def doc_codes(doc_lengths, first, rows):
    position = first + jnp.arange(rows, dtype=jnp.int32)
    ends = jnp.cumsum(doc_lengths)
    doc = jnp.sum((ends[None, :] <= position[:, None]).astype(jnp.int32), axis=1)
    high, low = doc // 8, doc % 8
    lane = (jnp.arange(2 * CODE, dtype=jnp.int32) % CODE)[None, :]
    hot = (lane == high[:, None]) | (lane == 32 + low[:, None])
    used = (lane < 16) | ((lane >= 32) & (lane < 40))
    inside = (position >= 0)[:, None]
    query_code = jnp.where(hot, 1.0, 0.0).astype(jnp.bfloat16)
    key_code = jnp.where(used & ~(hot & inside), FAR, 0.0).astype(jnp.bfloat16)
    return query_code, key_code


def first_tiles(doc_lengths, block_start, block_rows):
    starts = jnp.cumsum(doc_lengths) - doc_lengths
    position = block_start + TILE * jnp.arange(block_rows // TILE, dtype=jnp.int32)
    before = starts[None, :] <= position[:, None]
    first_key = jnp.max(jnp.where(before, starts[None, :], 0), axis=1)
    return (first_key - (block_start - block_rows)) // TILE


def spread_kernel(latent_ref, copies_ref):
    rows = latent_ref.shape[0]
    half = rows // 2
    rope = latent_ref[:, LATENT:]
    chunks = [latent_ref[:, i * 128 : (i + 1) * 128] for i in range(CHUNKS)]
    packed = jnp.concatenate(chunks + [jnp.concatenate([rope[:half], rope[half:]], axis=1)], axis=0)
    for i in range(copies_ref.shape[0]):
        copies_ref[i] = packed


def spread(latent, count):
    rows = latent.shape[0]
    vmem = pl.BlockSpec(memory_space=pltpu.VMEM)
    return pl.pallas_call(
        spread_kernel,
        in_specs=[vmem],
        out_specs=vmem,
        out_shape=jax.ShapeDtypeStruct((count, rows * CHUNKS + rows // 2, 128), latent.dtype),
        compiler_params=pltpu.CompilerParams(vmem_limit_bytes=16 * MIB),
        name="spread",
    )(latent)


def lift_tile(packed, code, key_up, value_up):
    count, rows = packed.shape[0], packed.shape[1] * 2 // (2 * CHUNKS + 1)
    chunks = [
        packed[:, i * rows : (i + 1) * rows].reshape(count * rows, 128) for i in range(CHUNKS)
    ]
    compact = jnp.concatenate(chunks, axis=1)
    ropes = packed[:, CHUNKS * rows :].reshape(count * rows // 2, 128)
    low = lax.broadcasted_iota(jnp.int32, ropes.shape, 1) < ROPE
    other = jnp.concatenate([ropes[:, ROPE:], ropes[:, :ROPE]], axis=1)
    firsts = jnp.where(low, ropes, other).reshape(count, rows // 2, 128)
    seconds = jnp.where(low, other, ropes).reshape(count, rows // 2, 128)
    rope = jnp.concatenate([firsts, seconds], axis=1).reshape(count * rows, 128)
    keys = jnp.dot(compact, key_up, preferred_element_type=jnp.float32).astype(jnp.bfloat16)
    values = jnp.dot(compact, value_up, preferred_element_type=jnp.float32).astype(jnp.bfloat16)
    left = lax.broadcasted_iota(jnp.int32, rope.shape, 1) < CODE
    columns = []
    for head in range(keys.shape[1] // NOPE):
        key = keys[:, head * NOPE : (head + 1) * NOPE]
        if head % 2 == 0:
            columns += [key, jnp.where(left, rope, code)]
        else:
            turned = jnp.concatenate([key[:, CODE:], key[:, :CODE]], axis=1)
            columns += [jnp.where(left, code, turned), jnp.where(left, turned, rope)]
    return columns, values


def lift_kernel(packed_ref, code_ref, key_up_ref, value_up_ref, rows_ref):
    columns, values = lift_tile(packed_ref[...], code_ref[...], key_up_ref[...], value_up_ref[...])
    for i, column in enumerate(columns):
        rows_ref[:, i * 128 : (i + 1) * 128] = column
    rows_ref[:, len(columns) * 128 :] = values


def lift(packed, code, key_up, value_up):
    rows = code.shape[0]
    steps = rows // TILE
    key_cols, value_cols = 2 * key_up.shape[1], value_up.shape[1]
    tiled = lambda cols: pl.BlockSpec((TILE, cols), lambda i: (i, 0))
    whole = lambda a: pl.BlockSpec(a.shape, lambda i: (0, 0))
    packed_spec = pl.BlockSpec((packed.shape[0] // steps,) + packed.shape[1:], lambda i: (i, 0, 0))
    return pl.pallas_call(
        lift_kernel,
        grid=(steps,),
        in_specs=[packed_spec, tiled(2 * CODE), whole(key_up), whole(value_up)],
        out_specs=tiled(key_cols + value_cols),
        out_shape=jax.ShapeDtypeStruct((rows, key_cols + value_cols), jnp.bfloat16),
        compiler_params=pltpu.CompilerParams(vmem_limit_bytes=60 * MIB),
        cost_estimate=pl.CostEstimate(
            flops=2 * rows * LATENT * (key_cols + value_cols),
            bytes_accessed=2 * rows * (key_cols + value_cols + 768),
            transcendentals=0,
        ),
        name="lift",
    )(packed, code, key_up, value_up)


def attend_kernel(
    first_ref, query_hbm, code_hbm, far_hbm, near_hbm, prev_code_hbm, key_up_hbm, value_up_hbm, own_hbm,
    out_hbm, query_ref, code_ref, prev_ref, prev_code_ref, key_up_ref, value_up_ref,
    key_ref, value_ref, out_ref, key_sems, value_sems, query_sems, out_sems, lift_sems, prev_sems,
    code_sem,
):
    tiles = query_ref.shape[0] // TILE
    heads = value_ref.shape[1] // VDIM
    key_cols = key_ref.shape[1]
    to_log2 = math.log2(math.e) / math.sqrt(HEAD)
    first_tile = first_ref[0]

    def tile_rows(tile):
        return pl.ds(pl.multiple_of(tile * TILE, TILE), TILE)

    def key_copies(tile):
        here, there = tile_rows(tile), tile_rows(tiles + tile)
        return (
            pltpu.make_async_copy(
                own_hbm.at[here, :key_cols], key_ref.at[there], key_sems.at[tile]
            ),
            pltpu.make_async_copy(
                own_hbm.at[here, key_cols:], value_ref.at[there], value_sems.at[tile]
            ),
        )

    def query_copy(tile):
        here = tile_rows(tile)
        return pltpu.make_async_copy(query_hbm.at[here], query_ref.at[here], query_sems.at[tile])

    def out_copy(tile):
        here = tile_rows(tile)
        return pltpu.make_async_copy(out_ref.at[here], out_hbm.at[here], out_sems.at[tile])

    share = prev_ref.shape[0] // tiles

    odd = first_ref[tiles] == 1

    def prev_copy(source, tile):
        here = pl.ds(tile * share, share)
        return pltpu.make_async_copy(source.at[here], prev_ref.at[here], prev_sems.at[tile])

    lift_copies = [
        pltpu.make_async_copy(source, target, lift_sems.at[i])
        for i, (source, target) in enumerate(
            [(key_up_hbm, key_up_ref), (value_up_hbm, value_up_ref), (prev_code_hbm, prev_code_ref)]
        )
    ]
    code_copy = pltpu.make_async_copy(code_hbm, code_ref, code_sem)

    @pl.when(first_tile < tiles)
    def _():
        for copy in lift_copies:
            copy.start()
        for tile in range(tiles):
            needed = first_tile <= tile
            pl.when(needed & odd)(lambda tile=tile: prev_copy(near_hbm, tile).start())
            pl.when(needed & ~odd)(lambda tile=tile: prev_copy(far_hbm, tile).start())

    code_copy.start()
    for tile in range(tiles):
        query_copy(tile).start()
        for copy in key_copies(tile):
            copy.start()

    @pl.when(first_tile < tiles)
    def _():
        for copy in lift_copies:
            copy.wait()

    @pl.loop(jnp.minimum(first_tile, tiles), tiles)
    def _(tile):
        prev_copy(near_hbm, tile).wait()
        rows = tile_rows(tile)
        packed = prev_ref[pl.ds(tile * share, share)]
        columns, values = lift_tile(packed, prev_code_ref[rows, :], key_up_ref[...], value_up_ref[...])
        for i, column in enumerate(columns):
            key_ref[rows, i * 128 : (i + 1) * 128] = column
        value_ref[rows, :] = values

    left = lax.broadcasted_iota(jnp.int32, (TILE, 128), 1) < CODE
    causal = lax.broadcasted_iota(jnp.int32, (TILE, TILE), 1) <= lax.broadcasted_iota(
        jnp.int32, (TILE, TILE), 0
    )

    def score(head, rows, span, code):
        at = head // 2 * PAIR
        middle = query_ref[rows, at + 128 : at + 256]
        if head % 2 == 0:
            query = [query_ref[rows, at : at + 128], jnp.where(left, middle, code)]
        else:
            query = [jnp.where(left, code, middle), query_ref[rows, at + 256 : at + 384]]
        return lax.dot_general(
            jnp.concatenate(query, axis=1),
            key_ref[span, head * 256 : (head + 1) * 256],
            (((1,), (1,)), ((), ())),
            preferred_element_type=jnp.float32,
        )

    def weigh(scores):
        far = scores.shape[1] - TILE
        own = jnp.where(causal, scores[:, far:], FAR)
        scores = jnp.concatenate([scores[:, :far], own], axis=1) if far else own
        top = jnp.max(scores, axis=1, keepdims=True) * to_log2
        return jnp.exp2(scores * to_log2 - top).astype(jnp.bfloat16)

    def attend_rows(step, count):
        rows = tile_rows(step)
        span = pl.ds(pl.multiple_of((tiles + 1 + step - count) * TILE, TILE), count * TILE)
        code = code_ref[rows, :]
        scores = [score(head, rows, span, code) for head in range(heads)]
        weights = [weigh(s) for s in scores]
        for head in range(heads):
            cols = slice(head * VDIM, (head + 1) * VDIM)
            ones = jnp.ones((count * TILE, VDIM), jnp.bfloat16)
            values = jnp.concatenate([value_ref[span, cols], ones], axis=1)
            total = jnp.dot(weights[head], values, preferred_element_type=jnp.float32)
            out_ref[rows, cols] = (total[:, :VDIM] / total[:, VDIM:]).astype(jnp.bfloat16)

    code_copy.wait()

    @pl.loop(0, tiles)
    def _(step):
        for tile in range(tiles):

            @pl.when(step == tile)
            def _():
                query_copy(tile).wait()
                for copy in key_copies(tile):
                    copy.wait()

        count = tiles + 1 + step - first_ref[step]
        for n in range(1, tiles + 2):
            pl.when(count == n)(functools.partial(attend_rows, step, n))
        out_copy(step).start()

    for tile in range(tiles):
        out_copy(tile).wait()


def attend(first, query, code, near, far, prev_code, key_up, value_up, own):
    rows, value_cols = own.shape[0], value_up.shape[1]
    key_cols = own.shape[1] - value_cols
    tiles = rows // TILE
    there = pl.BlockSpec(memory_space=pl.ANY)
    scratch = lambda *shape: pltpu.VMEM(shape, jnp.bfloat16)
    return pl.pallas_call(
        attend_kernel,
        in_specs=[pl.BlockSpec(memory_space=pltpu.SMEM)] + [there] * 8,
        out_specs=there,
        out_shape=jax.ShapeDtypeStruct((rows, value_cols), jnp.bfloat16),
        scratch_shapes=[
            scratch(*query.shape),
            scratch(*code.shape),
            scratch(*near.shape),
            scratch(*prev_code.shape),
            scratch(*key_up.shape),
            scratch(*value_up.shape),
            scratch(2 * rows, key_cols),
            scratch(2 * rows, value_cols),
            scratch(rows, value_cols),
            pltpu.SemaphoreType.DMA((tiles,)),
            pltpu.SemaphoreType.DMA((tiles,)),
            pltpu.SemaphoreType.DMA((tiles,)),
            pltpu.SemaphoreType.DMA((tiles,)),
            pltpu.SemaphoreType.DMA((3,)),
            pltpu.SemaphoreType.DMA((tiles,)),
            pltpu.SemaphoreType.DMA,
        ],
        compiler_params=pltpu.CompilerParams(vmem_limit_bytes=50 * MIB),
        cost_estimate=pl.CostEstimate(
            flops=8 * rows * rows * key_cols,
            bytes_accessed=2 * rows * (2 * key_cols + 4 * value_cols),
            transcendentals=rows * rows * 4,
        ),
        name="attend",
    )(first, query, code, far, near, prev_code, key_up, value_up, own)


def per_device(queries, latent, key_up, value_up, doc_lengths):
    uly_count = lax.axis_size("uly")
    own_rows = queries.shape[0]
    block_rows = own_rows * uly_count
    heads_dev = key_up.shape[1] // NOPE
    block_start = lax.axis_index("ctx") * block_rows
    ctx = lax.axis_index("ctx")
    parity = (ctx % 2).astype(jnp.int32)

    def prepare(lengths, rows):
        parts = rows.reshape(own_rows, uly_count, -1).transpose(1, 0, 2)
        codes = doc_codes(lengths, block_start - block_rows, 2 * block_rows)
        first = first_tiles(lengths, block_start, block_rows)
        return parts, codes[0][block_rows:], codes[1], jnp.concatenate([first, parity[None]])

    late = (parity == 1) & (ctx > 1)
    shapes = jax.eval_shape(prepare, doc_lengths, queries)
    skip = lambda *_: tuple(jnp.zeros(a.shape, a.dtype) for a in shapes)
    early = lax.cond(late, prepare, skip, doc_lengths, queries)
    latent, early = lax.optimization_barrier((latent, early))

    own = lax.all_to_all(spread(latent, uly_count), "uly", split_axis=0, concat_axis=0)
    parts, query_code, key_code, first = lax.cond(
        late, lambda held, *_: held, lambda _, *given: prepare(*given), early, doc_lengths, queries
    )
    ctx_count = lax.axis_size("ctx")
    far = passed_along(own, "ctx", range(1, ctx_count, 2))
    near = passed_along(own, "ctx", range(0, ctx_count, 2))
    local_query = lax.all_to_all(parts, "uly", split_axis=0, concat_axis=0)
    local_query = local_query.reshape(block_rows, -1)
    own_rows_lifted = lift(own, key_code[block_rows:], key_up, value_up)
    result = attend(
        first, local_query, query_code, near, far, key_code[:block_rows], key_up, value_up,
        own_rows_lifted,
    )
    result = result.reshape(uly_count, own_rows, heads_dev * VDIM)
    result = lax.all_to_all(result, "uly", split_axis=0, concat_axis=0)
    return jnp.transpose(result, (1, 0, 2)).reshape(own_rows, uly_count * heads_dev * VDIM)


def solution(mesh):
    placed = (P(("ctx", "uly"), None), P(("ctx", "uly"), None), P(None, "uly"), P(None, "uly"), P())
    return jax.shard_map(
        per_device, mesh=mesh, in_specs=placed, out_specs=P(("ctx", "uly"), None), check_vma=False
    )
```

```python
import functools
import math

import jax
import jax.numpy as jnp
from jax import lax
from jax.experimental import pallas as pl
from jax.experimental.pallas import tpu as pltpu
from jax.sharding import PartitionSpec as P

LATENT = 512
ROPE = 64
NOPE = 128
VDIM = 128
HEAD = NOPE + ROPE
PAIR = 2 * HEAD
CHUNKS = LATENT // 128
TILE = 256
CODE = 64
FAR = -(2.0**40)
MIB = 1 << 20


def passed_along(block, axis, senders):
    last = lax.axis_size(axis) - 1
    return lax.ppermute(block, axis, [(i, i + 1) for i in senders if i < last])


def doc_codes(doc_lengths, first, rows):
    position = first + jnp.arange(rows, dtype=jnp.int32)
    ends = jnp.cumsum(doc_lengths)
    doc = jnp.sum((ends[None, :] <= position[:, None]).astype(jnp.int32), axis=1)
    high, low = doc // 8, doc % 8
    lane = (jnp.arange(2 * CODE, dtype=jnp.int32) % CODE)[None, :]
    hot = (lane == high[:, None]) | (lane == 32 + low[:, None])
    used = (lane < 16) | ((lane >= 32) & (lane < 40))
    inside = (position >= 0)[:, None]
    query_code = jnp.where(hot, 1.0, 0.0).astype(jnp.bfloat16)
    key_code = jnp.where(used & ~(hot & inside), FAR, 0.0).astype(jnp.bfloat16)
    return query_code, key_code


def first_tiles(doc_lengths, block_start, block_rows):
    starts = jnp.cumsum(doc_lengths) - doc_lengths
    position = block_start + TILE * jnp.arange(block_rows // TILE, dtype=jnp.int32)
    before = starts[None, :] <= position[:, None]
    first_key = jnp.max(jnp.where(before, starts[None, :], 0), axis=1)
    return (first_key - (block_start - block_rows)) // TILE


def spread_kernel(latent_ref, copies_ref):
    rows = latent_ref.shape[0]
    half = rows // 2
    rope = latent_ref[:, LATENT:]
    chunks = [latent_ref[:, i * 128 : (i + 1) * 128] for i in range(CHUNKS)]
    packed = jnp.concatenate(chunks + [jnp.concatenate([rope[:half], rope[half:]], axis=1)], axis=0)
    for i in range(copies_ref.shape[0]):
        copies_ref[i] = packed


def spread(latent, count):
    rows = latent.shape[0]
    vmem = pl.BlockSpec(memory_space=pltpu.VMEM)
    return pl.pallas_call(
        spread_kernel,
        in_specs=[vmem],
        out_specs=vmem,
        out_shape=jax.ShapeDtypeStruct((count, rows * CHUNKS + rows // 2, 128), latent.dtype),
        compiler_params=pltpu.CompilerParams(vmem_limit_bytes=16 * MIB),
        name="spread",
    )(latent)


def lift_tile(packed, code, key_up, value_up):
    count, rows = packed.shape[0], packed.shape[1] * 2 // (2 * CHUNKS + 1)
    chunks = [
        packed[:, i * rows : (i + 1) * rows].reshape(count * rows, 128) for i in range(CHUNKS)
    ]
    compact = jnp.concatenate(chunks, axis=1)
    ropes = packed[:, CHUNKS * rows :].reshape(count * rows // 2, 128)
    low = lax.broadcasted_iota(jnp.int32, ropes.shape, 1) < ROPE
    other = jnp.concatenate([ropes[:, ROPE:], ropes[:, :ROPE]], axis=1)
    firsts = jnp.where(low, ropes, other).reshape(count, rows // 2, 128)
    seconds = jnp.where(low, other, ropes).reshape(count, rows // 2, 128)
    rope = jnp.concatenate([firsts, seconds], axis=1).reshape(count * rows, 128)
    keys = jnp.dot(compact, key_up, preferred_element_type=jnp.float32).astype(jnp.bfloat16)
    values = jnp.dot(compact, value_up, preferred_element_type=jnp.float32).astype(jnp.bfloat16)
    left = lax.broadcasted_iota(jnp.int32, rope.shape, 1) < CODE
    columns = []
    for head in range(keys.shape[1] // NOPE):
        key = keys[:, head * NOPE : (head + 1) * NOPE]
        if head % 2 == 0:
            columns += [key, jnp.where(left, rope, code)]
        else:
            turned = jnp.concatenate([key[:, CODE:], key[:, :CODE]], axis=1)
            columns += [jnp.where(left, code, turned), jnp.where(left, turned, rope)]
    return columns, values


def lift_kernel(packed_ref, code_ref, key_up_ref, value_up_ref, rows_ref):
    columns, values = lift_tile(packed_ref[...], code_ref[...], key_up_ref[...], value_up_ref[...])
    for i, column in enumerate(columns):
        rows_ref[:, i * 128 : (i + 1) * 128] = column
    rows_ref[:, len(columns) * 128 :] = values


def lift(packed, code, key_up, value_up):
    rows = code.shape[0]
    steps = rows // TILE
    key_cols, value_cols = 2 * key_up.shape[1], value_up.shape[1]
    tiled = lambda cols: pl.BlockSpec((TILE, cols), lambda i: (i, 0))
    whole = lambda a: pl.BlockSpec(a.shape, lambda i: (0, 0))
    packed_spec = pl.BlockSpec((packed.shape[0] // steps,) + packed.shape[1:], lambda i: (i, 0, 0))
    return pl.pallas_call(
        lift_kernel,
        grid=(steps,),
        in_specs=[packed_spec, tiled(2 * CODE), whole(key_up), whole(value_up)],
        out_specs=tiled(key_cols + value_cols),
        out_shape=jax.ShapeDtypeStruct((rows, key_cols + value_cols), jnp.bfloat16),
        compiler_params=pltpu.CompilerParams(vmem_limit_bytes=60 * MIB),
        cost_estimate=pl.CostEstimate(
            flops=2 * rows * LATENT * (key_cols + value_cols),
            bytes_accessed=2 * rows * (key_cols + value_cols + 768),
            transcendentals=0,
        ),
        name="lift",
    )(packed, code, key_up, value_up)


def attend_kernel(
    first_ref, query_hbm, code_hbm, far_hbm, near_hbm, prev_code_hbm, key_up_hbm, value_up_hbm, own_hbm,
    out_ref, query_ref, code_ref, prev_ref, prev_code_ref, key_up_ref, value_up_ref,
    key_ref, value_ref, key_sems, value_sems, query_sems, lift_sems, prev_sems,
    code_sem,
):
    tiles = query_ref.shape[0] // TILE
    heads = value_ref.shape[1] // VDIM
    key_cols = key_ref.shape[1]
    to_log2 = math.log2(math.e) / math.sqrt(HEAD)
    first_tile = first_ref[0]

    def tile_rows(tile):
        return pl.ds(pl.multiple_of(tile * TILE, TILE), TILE)

    def key_copies(tile):
        here, there = tile_rows(tile), tile_rows(tiles + tile)
        return (
            pltpu.make_async_copy(
                own_hbm.at[here, :key_cols], key_ref.at[there], key_sems.at[tile]
            ),
            pltpu.make_async_copy(
                own_hbm.at[here, key_cols:], value_ref.at[there], value_sems.at[tile]
            ),
        )

    def query_copy(tile):
        here = tile_rows(tile)
        return pltpu.make_async_copy(query_hbm.at[here], query_ref.at[here], query_sems.at[tile])

    share = prev_ref.shape[0] // tiles

    odd = first_ref[tiles] == 1

    def prev_copy(source, tile):
        here = pl.ds(tile * share, share)
        return pltpu.make_async_copy(source.at[here], prev_ref.at[here], prev_sems.at[tile])

    lift_copies = [
        pltpu.make_async_copy(source, target, lift_sems.at[i])
        for i, (source, target) in enumerate(
            [(key_up_hbm, key_up_ref), (value_up_hbm, value_up_ref), (prev_code_hbm, prev_code_ref)]
        )
    ]
    code_copy = pltpu.make_async_copy(code_hbm, code_ref, code_sem)

    @pl.when(first_tile < tiles)
    def _():
        for copy in lift_copies:
            copy.start()
        for tile in range(tiles):
            needed = first_tile <= tile
            pl.when(needed & odd)(lambda tile=tile: prev_copy(near_hbm, tile).start())
            pl.when(needed & ~odd)(lambda tile=tile: prev_copy(far_hbm, tile).start())

    code_copy.start()
    for tile in range(tiles):
        query_copy(tile).start()
        for copy in key_copies(tile):
            copy.start()

    @pl.when(first_tile < tiles)
    def _():
        for copy in lift_copies:
            copy.wait()

    @pl.loop(jnp.minimum(first_tile, tiles), tiles)
    def _(tile):
        prev_copy(near_hbm, tile).wait()
        rows = tile_rows(tile)
        packed = prev_ref[pl.ds(tile * share, share)]
        columns, values = lift_tile(packed, prev_code_ref[rows, :], key_up_ref[...], value_up_ref[...])
        for i, column in enumerate(columns):
            key_ref[rows, i * 128 : (i + 1) * 128] = column
        value_ref[rows, :] = values

    left = lax.broadcasted_iota(jnp.int32, (TILE, 128), 1) < CODE
    causal = lax.broadcasted_iota(jnp.int32, (TILE, TILE), 1) <= lax.broadcasted_iota(
        jnp.int32, (TILE, TILE), 0
    )

    def score(head, rows, span, code):
        at = head // 2 * PAIR
        middle = query_ref[rows, at + 128 : at + 256]
        if head % 2 == 0:
            query = [query_ref[rows, at : at + 128], jnp.where(left, middle, code)]
        else:
            query = [jnp.where(left, code, middle), query_ref[rows, at + 256 : at + 384]]
        return lax.dot_general(
            jnp.concatenate(query, axis=1),
            key_ref[span, head * 256 : (head + 1) * 256],
            (((1,), (1,)), ((), ())),
            preferred_element_type=jnp.float32,
        )

    def weigh(scores):
        far = scores.shape[1] - TILE
        own = jnp.where(causal, scores[:, far:], FAR)
        scores = jnp.concatenate([scores[:, :far], own], axis=1) if far else own
        top = jnp.max(scores, axis=1, keepdims=True) * to_log2
        return jnp.exp2(scores * to_log2 - top).astype(jnp.bfloat16)

    def attend_rows(step, count):
        rows = tile_rows(step)
        span = pl.ds(pl.multiple_of((tiles + 1 + step - count) * TILE, TILE), count * TILE)
        code = code_ref[rows, :]
        scores = [score(head, rows, span, code) for head in range(heads)]
        weights = [weigh(s) for s in scores]
        for head in range(heads):
            cols = slice(head * VDIM, (head + 1) * VDIM)
            ones = jnp.ones((count * TILE, VDIM), jnp.bfloat16)
            values = jnp.concatenate([value_ref[span, cols], ones], axis=1)
            total = jnp.dot(weights[head], values, preferred_element_type=jnp.float32)
            out_ref[rows, cols] = (total[:, :VDIM] / total[:, VDIM:]).astype(jnp.bfloat16)

    code_copy.wait()

    @pl.loop(0, tiles)
    def _(step):
        for tile in range(tiles):

            @pl.when(step == tile)
            def _():
                query_copy(tile).wait()
                for copy in key_copies(tile):
                    copy.wait()

        count = tiles + 1 + step - first_ref[step]
        for n in range(1, tiles + 2):
            pl.when(count == n)(functools.partial(attend_rows, step, n))


def attend(first, query, code, near, far, prev_code, key_up, value_up, own):
    rows, value_cols = own.shape[0], value_up.shape[1]
    key_cols = own.shape[1] - value_cols
    tiles = rows // TILE
    there = pl.BlockSpec(memory_space=pl.ANY)
    scratch = lambda *shape: pltpu.VMEM(shape, jnp.bfloat16)
    return pl.pallas_call(
        attend_kernel,
        in_specs=[pl.BlockSpec(memory_space=pltpu.SMEM)] + [there] * 8,
        out_specs=pl.BlockSpec(memory_space=pltpu.VMEM),
        out_shape=jax.ShapeDtypeStruct((rows, value_cols), jnp.bfloat16),
        scratch_shapes=[
            scratch(*query.shape),
            scratch(*code.shape),
            scratch(*near.shape),
            scratch(*prev_code.shape),
            scratch(*key_up.shape),
            scratch(*value_up.shape),
            scratch(2 * rows, key_cols),
            scratch(2 * rows, value_cols),
            pltpu.SemaphoreType.DMA((tiles,)),
            pltpu.SemaphoreType.DMA((tiles,)),
            pltpu.SemaphoreType.DMA((tiles,)),
            pltpu.SemaphoreType.DMA((3,)),
            pltpu.SemaphoreType.DMA((tiles,)),
            pltpu.SemaphoreType.DMA,
        ],
        compiler_params=pltpu.CompilerParams(vmem_limit_bytes=50 * MIB),
        cost_estimate=pl.CostEstimate(
            flops=8 * rows * rows * key_cols,
            bytes_accessed=2 * rows * (2 * key_cols + 4 * value_cols),
            transcendentals=rows * rows * 4,
        ),
        name="attend",
    )(first, query, code, far, near, prev_code, key_up, value_up, own)


def per_device(queries, latent, key_up, value_up, doc_lengths):
    uly_count = lax.axis_size("uly")
    own_rows = queries.shape[0]
    block_rows = own_rows * uly_count
    heads_dev = key_up.shape[1] // NOPE
    block_start = lax.axis_index("ctx") * block_rows
    ctx = lax.axis_index("ctx")
    parity = (ctx % 2).astype(jnp.int32)

    def prepare(lengths, rows):
        parts = rows.reshape(own_rows, uly_count, -1).transpose(1, 0, 2)
        codes = doc_codes(lengths, block_start - block_rows, 2 * block_rows)
        first = first_tiles(lengths, block_start, block_rows)
        return parts, codes[0][block_rows:], codes[1], jnp.concatenate([first, parity[None]])

    late = (parity == 1) & (ctx > 1)
    shapes = jax.eval_shape(prepare, doc_lengths, queries)
    skip = lambda *_: tuple(jnp.zeros(a.shape, a.dtype) for a in shapes)
    early = lax.cond(late, prepare, skip, doc_lengths, queries)
    latent, early = lax.optimization_barrier((latent, early))

    own = lax.all_to_all(spread(latent, uly_count), "uly", split_axis=0, concat_axis=0)
    parts, query_code, key_code, first = lax.cond(
        late, lambda held, *_: held, lambda _, *given: prepare(*given), early, doc_lengths, queries
    )
    ctx_count = lax.axis_size("ctx")
    far = passed_along(own, "ctx", range(1, ctx_count, 2))
    near = passed_along(own, "ctx", range(0, ctx_count, 2))
    local_query = lax.all_to_all(parts, "uly", split_axis=0, concat_axis=0)
    local_query = local_query.reshape(block_rows, -1)
    own_rows_lifted = lift(own, key_code[block_rows:], key_up, value_up)
    result = attend(
        first, local_query, query_code, near, far, key_code[:block_rows], key_up, value_up,
        own_rows_lifted,
    )
    result = result.reshape(uly_count, own_rows, heads_dev * VDIM)
    result = lax.all_to_all(result, "uly", split_axis=0, concat_axis=0)
    return jnp.transpose(result, (1, 0, 2)).reshape(own_rows, uly_count * heads_dev * VDIM)


def solution(mesh):
    placed = (P(("ctx", "uly"), None), P(("ctx", "uly"), None), P(None, "uly"), P(None, "uly"), P())
    return jax.shard_map(
        per_device, mesh=mesh, in_specs=placed, out_specs=P(("ctx", "uly"), None), check_vma=False
    )
```

```python
import functools
import math

import jax
import jax.numpy as jnp
from jax import lax
from jax.experimental import pallas as pl
from jax.experimental.pallas import tpu as pltpu
from jax.sharding import PartitionSpec as P

LATENT = 512
ROPE = 64
NOPE = 128
VDIM = 128
HEAD = NOPE + ROPE
PAIR = 2 * HEAD
CHUNKS = LATENT // 128
TILE = 256
CODE = 64
FAR = -(2.0**40)
MIB = 1 << 20


def passed_along(block, axis, senders):
    last = lax.axis_size(axis) - 1
    return lax.ppermute(block, axis, [(i, i + 1) for i in senders if i < last])


def doc_codes(doc_lengths, first, rows):
    position = first + jnp.arange(rows, dtype=jnp.int32)
    ends = jnp.cumsum(doc_lengths)
    doc = jnp.sum((ends[None, :] <= position[:, None]).astype(jnp.int32), axis=1)
    high, low = doc // 8, doc % 8
    lane = (jnp.arange(2 * CODE, dtype=jnp.int32) % CODE)[None, :]
    hot = (lane == high[:, None]) | (lane == 32 + low[:, None])
    used = (lane < 16) | ((lane >= 32) & (lane < 40))
    inside = (position >= 0)[:, None]
    query_code = jnp.where(hot, 1.0, 0.0).astype(jnp.bfloat16)
    key_code = jnp.where(used & ~(hot & inside), FAR, 0.0).astype(jnp.bfloat16)
    return query_code, key_code


def first_tiles(doc_lengths, block_start, block_rows):
    starts = jnp.cumsum(doc_lengths) - doc_lengths
    position = block_start + TILE * jnp.arange(block_rows // TILE, dtype=jnp.int32)
    before = starts[None, :] <= position[:, None]
    first_key = jnp.max(jnp.where(before, starts[None, :], 0), axis=1)
    return (first_key - (block_start - block_rows)) // TILE


def spread_kernel(latent_ref, copies_ref):
    rows = latent_ref.shape[0]
    half = rows // 2
    rope = latent_ref[:, LATENT:]
    chunks = [latent_ref[:, i * 128 : (i + 1) * 128] for i in range(CHUNKS)]
    packed = jnp.concatenate(chunks + [jnp.concatenate([rope[:half], rope[half:]], axis=1)], axis=0)
    for i in range(copies_ref.shape[0]):
        copies_ref[i] = packed


def spread(latent, count):
    rows = latent.shape[0]
    vmem = pl.BlockSpec(memory_space=pltpu.VMEM)
    return pl.pallas_call(
        spread_kernel,
        in_specs=[vmem],
        out_specs=vmem,
        out_shape=jax.ShapeDtypeStruct((count, rows * CHUNKS + rows // 2, 128), latent.dtype),
        compiler_params=pltpu.CompilerParams(vmem_limit_bytes=16 * MIB),
        name="spread",
    )(latent)


def lift_tile(packed, code, key_up, value_up):
    count, rows = packed.shape[0], packed.shape[1] * 2 // (2 * CHUNKS + 1)
    chunks = [
        packed[:, i * rows : (i + 1) * rows].reshape(count * rows, 128) for i in range(CHUNKS)
    ]
    compact = jnp.concatenate(chunks, axis=1)
    ropes = packed[:, CHUNKS * rows :].reshape(count * rows // 2, 128)
    low = lax.broadcasted_iota(jnp.int32, ropes.shape, 1) < ROPE
    other = jnp.concatenate([ropes[:, ROPE:], ropes[:, :ROPE]], axis=1)
    firsts = jnp.where(low, ropes, other).reshape(count, rows // 2, 128)
    seconds = jnp.where(low, other, ropes).reshape(count, rows // 2, 128)
    rope = jnp.concatenate([firsts, seconds], axis=1).reshape(count * rows, 128)
    keys = jnp.dot(compact, key_up, preferred_element_type=jnp.float32).astype(jnp.bfloat16)
    values = jnp.dot(compact, value_up, preferred_element_type=jnp.float32).astype(jnp.bfloat16)
    left = lax.broadcasted_iota(jnp.int32, rope.shape, 1) < CODE
    columns = []
    for head in range(keys.shape[1] // NOPE):
        key = keys[:, head * NOPE : (head + 1) * NOPE]
        if head % 2 == 0:
            columns += [key, jnp.where(left, rope, code)]
        else:
            turned = jnp.concatenate([key[:, CODE:], key[:, :CODE]], axis=1)
            columns += [jnp.where(left, code, turned), jnp.where(left, turned, rope)]
    return columns, values


def lift_kernel(packed_ref, code_ref, key_up_ref, value_up_ref, rows_ref):
    columns, values = lift_tile(packed_ref[...], code_ref[...], key_up_ref[...], value_up_ref[...])
    for i, column in enumerate(columns):
        rows_ref[:, i * 128 : (i + 1) * 128] = column
    rows_ref[:, len(columns) * 128 :] = values


def lift(packed, code, key_up, value_up):
    rows = code.shape[0]
    steps = rows // TILE
    key_cols, value_cols = 2 * key_up.shape[1], value_up.shape[1]
    tiled = lambda cols: pl.BlockSpec((TILE, cols), lambda i: (i, 0))
    whole = lambda a: pl.BlockSpec(a.shape, lambda i: (0, 0))
    packed_spec = pl.BlockSpec((packed.shape[0] // steps,) + packed.shape[1:], lambda i: (i, 0, 0))
    return pl.pallas_call(
        lift_kernel,
        grid=(steps,),
        in_specs=[packed_spec, tiled(2 * CODE), whole(key_up), whole(value_up)],
        out_specs=tiled(key_cols + value_cols),
        out_shape=jax.ShapeDtypeStruct((rows, key_cols + value_cols), jnp.bfloat16),
        compiler_params=pltpu.CompilerParams(vmem_limit_bytes=60 * MIB),
        cost_estimate=pl.CostEstimate(
            flops=2 * rows * LATENT * (key_cols + value_cols),
            bytes_accessed=2 * rows * (key_cols + value_cols + 768),
            transcendentals=0,
        ),
        name="lift",
    )(packed, code, key_up, value_up)


def attend_kernel(
    first_ref, query_hbm, code_hbm, far_hbm, near_hbm, prev_code_hbm, key_up_hbm, value_up_hbm, own_hbm,
    out_ref, query_ref, code_ref, prev_ref, prev_code_ref, key_up_ref, value_up_ref,
    key_ref, value_ref, key_sems, value_sems, query_sems, lift_sems, prev_sems,
    code_sem,
):
    tiles = query_ref.shape[0] // TILE
    heads = value_ref.shape[1] // VDIM
    key_cols = key_ref.shape[1]
    to_log2 = math.log2(math.e) / math.sqrt(HEAD)
    first_tile = first_ref[0]

    def tile_rows(tile):
        return pl.ds(pl.multiple_of(tile * TILE, TILE), TILE)

    def key_copies(tile):
        here, there = tile_rows(tile), tile_rows(tiles + tile)
        return (
            pltpu.make_async_copy(
                own_hbm.at[here, :key_cols], key_ref.at[there], key_sems.at[tile]
            ),
            pltpu.make_async_copy(
                own_hbm.at[here, key_cols:], value_ref.at[there], value_sems.at[tile]
            ),
        )

    def query_copy(tile):
        here = tile_rows(tile)
        return pltpu.make_async_copy(query_hbm.at[here], query_ref.at[here], query_sems.at[tile])

    share = prev_ref.shape[0] // tiles

    odd = first_ref[tiles] == 1

    def prev_copy(source, tile):
        here = pl.ds(tile * share, share)
        return pltpu.make_async_copy(source.at[here], prev_ref.at[here], prev_sems.at[tile])

    lift_copies = [
        pltpu.make_async_copy(source, target, lift_sems.at[i])
        for i, (source, target) in enumerate(
            [(key_up_hbm, key_up_ref), (value_up_hbm, value_up_ref), (prev_code_hbm, prev_code_ref)]
        )
    ]
    code_copy = pltpu.make_async_copy(code_hbm, code_ref, code_sem)

    @pl.when(first_tile < tiles)
    def _():
        for tile in range(tiles):
            needed = first_tile <= tile
            pl.when(needed & odd)(lambda tile=tile: prev_copy(near_hbm, tile).start())
            pl.when(needed & ~odd)(lambda tile=tile: prev_copy(far_hbm, tile).start())
        for copy in lift_copies:
            copy.start()

    code_copy.start()
    for tile in range(tiles):
        query_copy(tile).start()
        for copy in key_copies(tile):
            copy.start()

    @pl.when(first_tile < tiles)
    def _():
        for copy in lift_copies:
            copy.wait()

    @pl.loop(jnp.minimum(first_tile, tiles), tiles)
    def _(tile):
        prev_copy(near_hbm, tile).wait()
        rows = tile_rows(tile)
        packed = prev_ref[pl.ds(tile * share, share)]
        columns, values = lift_tile(packed, prev_code_ref[rows, :], key_up_ref[...], value_up_ref[...])
        for i, column in enumerate(columns):
            key_ref[rows, i * 128 : (i + 1) * 128] = column
        value_ref[rows, :] = values

    left = lax.broadcasted_iota(jnp.int32, (TILE, 128), 1) < CODE
    causal = lax.broadcasted_iota(jnp.int32, (TILE, TILE), 1) <= lax.broadcasted_iota(
        jnp.int32, (TILE, TILE), 0
    )

    def score(head, rows, span, code):
        at = head // 2 * PAIR
        middle = query_ref[rows, at + 128 : at + 256]
        if head % 2 == 0:
            query = [query_ref[rows, at : at + 128], jnp.where(left, middle, code)]
        else:
            query = [jnp.where(left, code, middle), query_ref[rows, at + 256 : at + 384]]
        return lax.dot_general(
            jnp.concatenate(query, axis=1),
            key_ref[span, head * 256 : (head + 1) * 256],
            (((1,), (1,)), ((), ())),
            preferred_element_type=jnp.float32,
        )

    def weigh(scores):
        far = scores.shape[1] - TILE
        own = jnp.where(causal, scores[:, far:], FAR)
        scores = jnp.concatenate([scores[:, :far], own], axis=1) if far else own
        top = jnp.max(scores, axis=1, keepdims=True) * to_log2
        return jnp.exp2(scores * to_log2 - top).astype(jnp.bfloat16)

    def attend_rows(step, count):
        rows = tile_rows(step)
        span = pl.ds(pl.multiple_of((tiles + 1 + step - count) * TILE, TILE), count * TILE)
        code = code_ref[rows, :]
        scores = [score(head, rows, span, code) for head in range(heads)]
        weights = [weigh(s) for s in scores]
        for head in range(heads):
            cols = slice(head * VDIM, (head + 1) * VDIM)
            ones = jnp.ones((count * TILE, VDIM), jnp.bfloat16)
            values = jnp.concatenate([value_ref[span, cols], ones], axis=1)
            total = jnp.dot(weights[head], values, preferred_element_type=jnp.float32)
            out_ref[rows, cols] = (total[:, :VDIM] / total[:, VDIM:]).astype(jnp.bfloat16)

    code_copy.wait()

    @pl.loop(0, tiles)
    def _(step):
        for tile in range(tiles):

            @pl.when(step == tile)
            def _():
                query_copy(tile).wait()
                for copy in key_copies(tile):
                    copy.wait()

        count = tiles + 1 + step - first_ref[step]
        for n in range(1, tiles + 2):
            pl.when(count == n)(functools.partial(attend_rows, step, n))


def attend(first, query, code, near, far, prev_code, key_up, value_up, own):
    rows, value_cols = own.shape[0], value_up.shape[1]
    key_cols = own.shape[1] - value_cols
    tiles = rows // TILE
    there = pl.BlockSpec(memory_space=pl.ANY)
    scratch = lambda *shape: pltpu.VMEM(shape, jnp.bfloat16)
    return pl.pallas_call(
        attend_kernel,
        in_specs=[pl.BlockSpec(memory_space=pltpu.SMEM)] + [there] * 8,
        out_specs=pl.BlockSpec(memory_space=pltpu.VMEM),
        out_shape=jax.ShapeDtypeStruct((rows, value_cols), jnp.bfloat16),
        scratch_shapes=[
            scratch(*query.shape),
            scratch(*code.shape),
            scratch(*near.shape),
            scratch(*prev_code.shape),
            scratch(*key_up.shape),
            scratch(*value_up.shape),
            scratch(2 * rows, key_cols),
            scratch(2 * rows, value_cols),
            pltpu.SemaphoreType.DMA((tiles,)),
            pltpu.SemaphoreType.DMA((tiles,)),
            pltpu.SemaphoreType.DMA((tiles,)),
            pltpu.SemaphoreType.DMA((3,)),
            pltpu.SemaphoreType.DMA((tiles,)),
            pltpu.SemaphoreType.DMA,
        ],
        compiler_params=pltpu.CompilerParams(vmem_limit_bytes=50 * MIB),
        cost_estimate=pl.CostEstimate(
            flops=8 * rows * rows * key_cols,
            bytes_accessed=2 * rows * (2 * key_cols + 4 * value_cols),
            transcendentals=rows * rows * 4,
        ),
        name="attend",
    )(first, query, code, far, near, prev_code, key_up, value_up, own)


def per_device(queries, latent, key_up, value_up, doc_lengths):
    uly_count = lax.axis_size("uly")
    own_rows = queries.shape[0]
    block_rows = own_rows * uly_count
    heads_dev = key_up.shape[1] // NOPE
    block_start = lax.axis_index("ctx") * block_rows
    ctx = lax.axis_index("ctx")
    parity = (ctx % 2).astype(jnp.int32)

    def prepare(lengths, rows):
        parts = rows.reshape(own_rows, uly_count, -1).transpose(1, 0, 2)
        codes = doc_codes(lengths, block_start - block_rows, 2 * block_rows)
        first = first_tiles(lengths, block_start, block_rows)
        return parts, codes[0][block_rows:], codes[1], jnp.concatenate([first, parity[None]])

    late = (parity == 1) & (ctx > 1)
    shapes = jax.eval_shape(prepare, doc_lengths, queries)
    skip = lambda *_: tuple(jnp.zeros(a.shape, a.dtype) for a in shapes)
    early = lax.cond(late, prepare, skip, doc_lengths, queries)
    latent, early = lax.optimization_barrier((latent, early))

    own = lax.all_to_all(spread(latent, uly_count), "uly", split_axis=0, concat_axis=0)
    parts, query_code, key_code, first = lax.cond(
        late, lambda held, *_: held, lambda _, *given: prepare(*given), early, doc_lengths, queries
    )
    ctx_count = lax.axis_size("ctx")
    far = passed_along(own, "ctx", range(1, ctx_count, 2))
    near = passed_along(own, "ctx", range(0, ctx_count, 2))
    local_query = lax.all_to_all(parts, "uly", split_axis=0, concat_axis=0)
    local_query = local_query.reshape(block_rows, -1)
    own_rows_lifted = lift(own, key_code[block_rows:], key_up, value_up)
    result = attend(
        first, local_query, query_code, near, far, key_code[:block_rows], key_up, value_up,
        own_rows_lifted,
    )
    result = result.reshape(uly_count, own_rows, heads_dev * VDIM)
    result = lax.all_to_all(result, "uly", split_axis=0, concat_axis=0)
    return jnp.transpose(result, (1, 0, 2)).reshape(own_rows, uly_count * heads_dev * VDIM)


def solution(mesh):
    placed = (P(("ctx", "uly"), None), P(("ctx", "uly"), None), P(None, "uly"), P(None, "uly"), P())
    return jax.shard_map(
        per_device, mesh=mesh, in_specs=placed, out_specs=P(("ctx", "uly"), None), check_vma=False
    )
```
